128 devices in a mesh: dp: 4 (over z), seq: 8 (over x, core), mp: 4 (over y).
Axes of the slice: x: 4, y: 4, z: 4, core: 2. Of those that a mesh axis runs over, the one named last changes fastest.
Arguments:
- tokens: float32 [4, 4096, 1024], P('dp', 'seq'), may hold values from -6 to 6
- cotangent: float32 [4, 4096, 1024], P('dp', 'seq'), may hold values from -6 to 6
- in_weight: float32 [3, 1024, 1024], P(None, ('dp', 'seq'), 'mp'), may hold values from -0.1875 to 0.1875
- in_first: float32 [3, 1024, 1024], P(None, ('dp', 'seq'), 'mp'), may hold values from -80 to 80
- in_second: float32 [3, 1024, 1024], P(None, ('dp', 'seq'), 'mp'), may hold values from 425.984 to 6881.28
- out_weight: float32 [1024, 1024], P('mp', ('dp', 'seq')), may hold values from -0.1875 to 0.1875
- out_first: float32 [1024, 1024], P('mp', ('dp', 'seq')), may hold values from -80 to 80
- out_second: float32 [1024, 1024], P('mp', ('dp', 'seq')), may hold values from 425.984 to 6881.28
- gu_weight: float32 [2, 1024, 4608], P(None, ('dp', 'seq'), 'mp'), may hold values from -0.1875 to 0.1875
- gu_first: float32 [2, 1024, 4608], P(None, ('dp', 'seq'), 'mp'), may hold values from -24 to 24
- gu_second: float32 [2, 1024, 4608], P(None, ('dp', 'seq'), 'mp'), may hold values from 39.3216 to 622.592
- down_weight: float32 [4608, 1024], P('mp', ('dp', 'seq')), may hold values from -0.09375 to 0.09375
- down_first: float32 [4608, 1024], P('mp', ('dp', 'seq')), may hold values from -64 to 64
- down_second: float32 [4608, 1024], P('mp', ('dp', 'seq')), may hold values from 212.992 to 3440.64
- conv_weight: float32 [3, 1024], P(None, ('dp', 'seq')), may hold values from -3 to 3
- conv_first: float32 [3, 1024], P(None, ('dp', 'seq')), may hold values from -80 to 80
- conv_second: float32 [3, 1024], P(None, ('dp', 'seq')), may hold values from 425.984 to 6881.28
- norm_gains: float32 [2, 1024], P(None, ('dp', 'seq')), may hold values from 0.5 to 1.5
- gains_first: float32 [2, 1024], P(None, ('dp', 'seq')), may hold values from -80 to 80
- gains_second: float32 [2, 1024], P(None, ('dp', 'seq')), may hold values from 425.984 to 6881.28
Outputs:
- mixed: float32 [4, 4096, 1024], P('dp', 'seq')
- token_grad: float32 [4, 4096, 1024], P('dp', 'seq')
- in_master: float32 [3, 1024, 1024], P(None, ('dp', 'seq'), 'mp')
- in_moment: float32 [3, 1024, 1024], P(None, ('dp', 'seq'), 'mp')
- in_square: float32 [3, 1024, 1024], P(None, ('dp', 'seq'), 'mp')
- out_master: float32 [1024, 1024], P('mp', ('dp', 'seq'))
- out_moment: float32 [1024, 1024], P('mp', ('dp', 'seq'))
- out_square: float32 [1024, 1024], P('mp', ('dp', 'seq'))
- gu_master: float32 [2, 1024, 4608], P(None, ('dp', 'seq'), 'mp')
- gu_moment: float32 [2, 1024, 4608], P(None, ('dp', 'seq'), 'mp')
- gu_square: float32 [2, 1024, 4608], P(None, ('dp', 'seq'), 'mp')
- down_master: float32 [4608, 1024], P('mp', ('dp', 'seq'))
- down_moment: float32 [4608, 1024], P('mp', ('dp', 'seq'))
- down_square: float32 [4608, 1024], P('mp', ('dp', 'seq'))
- conv_master: float32 [3, 1024], P(None, ('dp', 'seq'))
- conv_moment: float32 [3, 1024], P(None, ('dp', 'seq'))
- conv_square: float32 [3, 1024], P(None, ('dp', 'seq'))
- gains_master: float32 [2, 1024], P(None, ('dp', 'seq'))
- gains_moment: float32 [2, 1024], P(None, ('dp', 'seq'))
- gains_square: float32 [2, 1024], P(None, ('dp', 'seq'))
The draws below stay inside these ranges and needn't reach their ends.
All inputs are finite; a program needn't handle non-finite values.
Results may differ from the reference program's by a relative error of at most 0.025.
Values may be sent and summed in bfloat16 or wider, within the bound.
A program may use at most 128 MiB of HBM per device.

```python
import math
import jax
import jax.numpy as jnp
from jax import lax

D = 1024
FF = 4608
SEQ_LEN = 4096
STEP = 10
SEQS = 4
TOTAL = 16384


def levels(own_key, shape, pieces, least, largest):
    factor_of = 1.0
    for position, blocks in pieces:
        steps = jax.random.uniform(jax.random.fold_in(jax.random.fold_in(own_key, 6), position), (blocks,), jnp.float32, least / len(pieces), largest / len(pieces))
        factor_of = factor_of * jnp.repeat(jnp.exp(steps), shape[position] // blocks).reshape((-1,) + (1,) * (len(shape) - 1 - position))
    return factor_of


def centred(key, extent, width, most, pieces=(), held_as=jnp.bfloat16):
    gain = levels(key, extent, pieces, -0.22, 0.18) if pieces else 1.0
    entries = jax.random.normal(key, extent, jnp.float32) * width * gain
    return jnp.minimum(jnp.maximum(entries, -most), most).astype(held_as)


def setup_inputs(seed: int = 0) -> dict:
    seeds = jax.random.split(jax.random.key(seed), 21)
    return {
        "tokens": centred(seeds[0], (SEQS, SEQ_LEN, D), 1.0, 6.0, ((0, 4), (1, 8)), jnp.float32),
        "cotangent": centred(seeds[1], (SEQS, SEQ_LEN, D), 1.0, 6.0, ((0, 4), (1, 8)), jnp.float32),
        "in_weight": centred(seeds[2], (3, D, D), D ** -0.5, 0.1875, ((1, 32), (2, 4)), jnp.float32),
        "in_first": centred(seeds[3], (3, D, D), (0.11 * TOTAL ** 0.5), 80.0, ((1, 32), (2, 4)), jnp.float32),
        "in_second": jnp.clip(jnp.exp(math.log(6881.28) - 2.7821581 * jax.random.uniform(seeds[4], (3, D, D), jnp.float32) ** levels(seeds[4], (3, D, D), ((1, 32), (2, 4)), -0.2, 0.2)), 425.984, 6881.28),
        "out_weight": centred(seeds[5], (D, D), D ** -0.5, 0.1875, ((0, 4), (1, 32)), jnp.float32),
        "out_first": centred(seeds[6], (D, D), (0.11 * TOTAL ** 0.5), 80.0, ((0, 4), (1, 32)), jnp.float32),
        "out_second": jnp.clip(jnp.exp(math.log(6881.28) - 2.7821581 * jax.random.uniform(seeds[7], (D, D), jnp.float32) ** levels(seeds[7], (D, D), ((0, 4), (1, 32)), -0.2, 0.2)), 425.984, 6881.28),
        "gu_weight": centred(seeds[8], (2, D, FF), D ** -0.5, 0.1875, ((1, 32), (2, 4)), jnp.float32),
        "gu_first": centred(seeds[9], (2, D, FF), (0.033 * TOTAL ** 0.5), 24.0, ((1, 32), (2, 4)), jnp.float32),
        "gu_second": jnp.clip(jnp.exp(math.log(622.592) - 2.7621173 * jax.random.uniform(seeds[10], (2, D, FF), jnp.float32) ** levels(seeds[10], (2, D, FF), ((1, 32), (2, 4)), -0.2, 0.2)), 39.3216, 622.592),
        "down_weight": centred(seeds[11], (FF, D), FF ** -0.5, 0.09375, ((0, 4), (1, 32)), jnp.float32),
        "down_first": centred(seeds[12], (FF, D), (0.077 * TOTAL ** 0.5), 64.0, ((0, 4), (1, 32)), jnp.float32),
        "down_second": jnp.clip(jnp.exp(math.log(3440.64) - 2.7821581 * jax.random.uniform(seeds[13], (FF, D), jnp.float32) ** levels(seeds[13], (FF, D), ((0, 4), (1, 32)), -0.2, 0.2)), 212.992, 3440.64),
        "conv_weight": centred(seeds[14], (3, D), 0.6, 3.0, ((1, 32),), jnp.float32),
        "conv_first": centred(seeds[15], (3, D), (0.11 * TOTAL ** 0.5), 80.0, ((1, 32),), jnp.float32),
        "conv_second": jnp.clip(jnp.exp(math.log(6881.28) - 2.7821581 * jax.random.uniform(seeds[16], (3, D), jnp.float32) ** levels(seeds[16], (3, D), ((1, 32),), -0.2, 0.2)), 425.984, 6881.28),
        "norm_gains": jnp.clip(1.0 + 0.1 * jax.random.normal(seeds[17], (2, D), jnp.float32), 0.5, 1.5),
        "gains_first": centred(seeds[18], (2, D), (0.11 * TOTAL ** 0.5), 80.0, ((1, 32),), jnp.float32),
        "gains_second": jnp.clip(jnp.exp(math.log(6881.28) - 2.7821581 * jax.random.uniform(seeds[19], (2, D), jnp.float32) ** levels(seeds[19], (2, D), ((1, 32),), -0.2, 0.2)), 425.984, 6881.28),
    }


beta_one = 0.9
beta_two = 0.95
eps_adam = 1e-08
eps_norm = 1e-05
rate_matrix = 0.05
rate_small = 0.3
decay_matrix = 0.1
highest = lax.Precision.HIGHEST

@jax.custom_vjp
def low(v):
    return lax.optimization_barrier(v.astype(jnp.bfloat16)).astype(jnp.float32)

@jax.custom_vjp
def low_back(v):
    return v

def low_keep(v):
    return (low(v), None)

def low_pass(kept, grad):
    return (grad,)

def back_keep(v):
    return (v, None)

def back_low(kept, grad):
    return (low(grad),)
low.defvjp(low_keep, low_pass)
low_back.defvjp(back_keep, back_low)

def rms_scale(values):
    return lax.rsqrt(lax.optimization_barrier(jnp.mean(values * values, axis=-1, keepdims=True)) + eps_norm)

def forward(sequence, in_weight, out_weight, gu_weight, down_weight, conv_weight, norm_gains):
    in_copy = low(in_weight)
    out_copy = low(out_weight)
    gu_copy = low(gu_weight)
    down_copy = low(down_weight)
    taps = low(conv_weight)
    gains = low(norm_gains)
    act_one = low(sequence * rms_scale(sequence) * gains[0])
    projected = jnp.einsum('ld,kde->kle', act_one, in_copy, precision=highest)
    bgate = low_back(projected[0])
    cgate = low_back(projected[1])
    xvalue = low_back(projected[2])
    mixed_in = low(bgate * xvalue)
    padded = jnp.pad(mixed_in, ((2, 0), (0, 0)))
    conv_out = taps[0] * padded[:-2] + taps[1] * padded[1:-1] + taps[2] * padded[2:]
    conv_out = low_back(conv_out)
    gated = low(cgate * conv_out)
    branch = low_back(jnp.dot(gated, out_copy, precision=highest))
    resid = sequence + branch
    act_two = low(resid * rms_scale(resid) * gains[1])
    gate_pre = low_back(jnp.dot(act_two, gu_copy[0], precision=highest))
    up_pre = low_back(jnp.dot(act_two, gu_copy[1], precision=highest))
    hidden = low(jax.nn.silu(gate_pre) * up_pre)
    ffn = low_back(jnp.dot(hidden, down_copy, precision=highest))
    return resid + ffn

def adamw(master, first, second, grad, rate, decay):
    moment = beta_one * first + (1.0 - beta_one) * grad
    square = beta_two * second + (1.0 - beta_two) * grad * grad
    moment_hat = moment / (1.0 - beta_one ** STEP)
    square_hat = square / (1.0 - beta_two ** STEP)
    renewed = master - rate * (moment_hat / (jnp.sqrt(square_hat) + eps_adam) + decay * master)
    return (renewed, moment, square)

def reference(tokens, cotangent, in_weight, in_first, in_second, out_weight, out_first, out_second, gu_weight, gu_first, gu_second, down_weight, down_first, down_second, conv_weight, conv_first, conv_second, norm_gains, gains_first, gains_second):
    params = (in_weight, out_weight, gu_weight, down_weight, conv_weight, norm_gains)

    def one_sequence(carry, pair):
        outputs, pullback = jax.vjp(forward, pair[0], *params)
        grads = pullback(pair[1])
        totals = tuple((total + grad for total, grad in zip(carry, grads[1:])))
        return (totals, (outputs, grads[0]))
    start = tuple((jnp.zeros_like(param) for param in params))
    totals, (mixed, token_grad) = lax.scan(one_sequence, start, (tokens, cotangent))
    in_new = adamw(in_weight, in_first, in_second, totals[0], rate_matrix, decay_matrix)
    out_new = adamw(out_weight, out_first, out_second, totals[1], rate_matrix, decay_matrix)
    gu_new = adamw(gu_weight, gu_first, gu_second, totals[2], rate_matrix, decay_matrix)
    down_new = adamw(down_weight, down_first, down_second, totals[3], rate_matrix, decay_matrix)
    conv_new = adamw(conv_weight, conv_first, conv_second, totals[4], rate_small, 0.0)
    gains_new = adamw(norm_gains, gains_first, gains_second, totals[5], rate_small, 0.0)
    return (mixed, token_grad, in_new[0], in_new[1], in_new[2], out_new[0], out_new[1], out_new[2], gu_new[0], gu_new[1], gu_new[2], down_new[0], down_new[1], down_new[2], conv_new[0], conv_new[1], conv_new[2], gains_new[0], gains_new[1], gains_new[2])
```

```python
import jax
import jax.numpy as jnp
from jax import lax
from jax.experimental import pallas as pl
from jax.experimental.pallas import tpu as pltpu
from jax.sharding import PartitionSpec as P

STEP = 10

beta_one = 0.9
beta_two = 0.95
eps_adam = 1e-08
eps_norm = 1e-05
rate_matrix = 0.05
rate_small = 0.3
decay_matrix = 0.1

MESH = pl.DeviceIdType.MESH
bf16 = jnp.bfloat16
f32 = jnp.float32

ROWS = 512
CHUNK = 128
D = 1024
CH = 256
FF = 1152
IN0, OUT0, SM0, GU0, DN0, COLS = 0, 768, 1024, 1152, 3456, 4608


def adamw(master, first, second, grad, rate, decay):
    moment = beta_one * first + (1.0 - beta_one) * grad
    square = beta_two * second + (1.0 - beta_two) * grad * grad
    moment_hat = moment / (1.0 - beta_one**STEP)
    square_hat = square / (1.0 - beta_two**STEP)
    renewed = master - rate * (moment_hat / (jnp.sqrt(square_hat) + eps_adam) + decay * master)
    return (renewed, moment, square)


def rms_scale(values):
    return lax.rsqrt(jnp.mean(values * values, axis=-1, keepdims=True) + eps_norm)


def dot_nn(a, b):
    return jnp.dot(a, b, preferred_element_type=f32)


def dot_nt(a, b):
    return lax.dot_general(a, b, (((1,), (1,)), ((), ())), preferred_element_type=f32)


def dot_tn(a, b):
    return lax.dot_general(a, b, (((0,), (0,)), ((), ())), preferred_element_type=f32)


N_SEMS = 128


def kernel(
    tok_h,
    cot_h,
    w_in,
    w_out,
    w_gu,
    w_dn,
    w_conv,
    w_gain,
    mixed_o,
    tg_o,
    g_in,
    g_out,
    g_gu,
    g_dn,
    small_o,
    tok,
    cot,
    htok,
    square,
    W,
    G,
    RC,
    RX,
    T,
    RZ,
    act1,
    ulow,
    act2,
    rlow,
    hid,
    GG,
    b_s,
    c_s,
    x_s,
    conv_s,
    xext,
    gext,
    mxb,
    gated,
    GB,
    hb,
    smw,
    SM,
    SMR,
    PY,
    RY,
    OWN,
    res_s,
    mixrow,
    tgrow,
    ssem,
    rsem,
    lsem,
):
    z = lax.axis_index("dp")
    seq = lax.axis_index("seq")
    y = lax.axis_index("mp")
    x = seq // 2
    c = lax.rem(seq, 2)
    oc = 1 - c

    def near(value, step):
        return lax.rem(value + step, 4)

    def to_x(step):
        return (z, near(x, step) * 2 + c, y)

    def to_z(step):
        return (near(z, step), seq, y)

    def to_y(step):
        return (z, seq, near(y, step))

    to_core = (z, x * 2 + oc, y)
    to_next = (z, lax.rem(seq + 1, 8), y)
    to_prev = (z, lax.rem(seq + 7, 8), y)

    counter = [0]
    pending = []

    def send(src, dst, where):
        i = counter[0]
        counter[0] += 1
        copy = pltpu.make_async_remote_copy(
            src, dst, ssem.at[i], rsem.at[i], device_id=where, device_id_type=MESH
        )
        copy.start()
        pending.append(copy)
        return copy

    def arrived(copies):
        for copy in copies:
            copy.wait_recv()

    barrier = pltpu.get_barrier_semaphore()
    peers = [to_core, to_next, to_prev]
    for step in (1, 2, 3):
        peers += [to_x(step), to_z(step), to_y(step)]
    for peer in peers:
        pl.semaphore_signal(barrier, inc=1, device_id=peer, device_id_type=MESH)
    load_tok = pltpu.make_async_copy(tok_h, tok, lsem.at[2])
    load_tok.start()
    load_cot = pltpu.make_async_copy(cot_h, cot, lsem.at[3])
    load_cot.start()

    for k in range(3):
        W[z, x, c, :, CH * k : CH * k + CH] = w_in[k].astype(bf16)
    W[z, x, c, :, OUT0:SM0] = w_out[...].T.astype(bf16)
    square[...] = jnp.zeros((128, 128), f32)
    square[0:3, 0:32] = w_conv[...]
    square[3:5, 0:32] = w_gain[...]
    W[z, x, c, :, SM0:GU0] = square[...].T[0:32].astype(bf16)
    for t in range(9):
        for k in range(2):
            at = GU0 + 256 * t + 128 * k
            W[z, x, c, :, at : at + 128] = w_gu[k, :, 128 * t : 128 * t + 128].astype(bf16)
    W[z, x, c, :, DN0:COLS] = w_dn[...].T.astype(bf16)
    pl.semaphore_wait(barrier, len(peers))

    def ag_one(lo, mid, hi):
        a, b = pl.ds(lo, mid - lo), pl.ds(mid, hi - mid)
        src_a, src_b = W.at[z, x, c, :, a], W.at[z, x, c, :, b]
        return (
            [send(src_a, src_a, to_x(s)) for s in (1, 3, 2)],
            [send(src_b, src_b, to_z(s)) for s in (1, 3, 2)],
        )

    def ag_two(copies, lo, mid, hi):
        a, b = pl.ds(lo, mid - lo), pl.ds(mid, hi - mid)
        src_a, src_b = W.at[z, :, c, :, a], W.at[:, x, c, :, b]
        arrived(copies[0])
        first = [send(src_a, src_a, to_z(s)) for s in (1, 3, 2)]
        arrived(copies[1])
        return first + [send(src_b, src_b, to_x(s)) for s in (1, 3, 2)]

    def ag_three(copies, lo, hi):
        arrived(copies)
        src = W.at[:, :, c, :, pl.ds(lo, hi - lo)]
        return [send(src, src, to_core)]

    g0 = (IN0, 640, GU0)
    g1 = (GU0, GU0 + 1152, DN0)
    g2 = (DN0, DN0 + 640, COLS)
    ag0 = ag_one(*g0)
    halo = send(tok_h.at[pl.ds(ROWS - 16, 16)], htok, to_next)
    load_cot.wait()
    for r in range(0, ROWS, 128):
        ulow[r : r + 128] = cot[r : r + 128].astype(bf16)
    ag0 = ag_two(ag0, *g0)
    ag1 = ag_one(*g1)
    ag2 = ag_one(*g2)
    ag0 = ag_three(ag0, IN0, GU0)
    ag1 = ag_two(ag1, *g1)
    ag2 = ag_two(ag2, *g2)
    arrived(ag0)

    def weights(lo, n):
        return W[:, :, :, :, pl.ds(lo, n)].reshape(D, n)

    def weight_rows(block, lo, n):
        return W[block, :, :, :, pl.ds(lo, n)].reshape(256, n)

    smw[...] = weights(SM0, 128).astype(f32).T[:8]
    gain_one = smw[3:4]
    gain_two = smw[4:5]
    own_channels = pl.ds(pl.multiple_of(y * CH, CH), CH)
    taps = smw[:, own_channels]
    tap0, tap1, tap2 = taps[0:1], taps[1:2], taps[2:3]

    def first_norm(v):
        return (v * rms_scale(v) * gain_one).astype(bf16)

    load_tok.wait()
    for r in range(0, ROWS, 128):
        act1[r + 16 : r + 144] = first_norm(tok[r : r + 128])
    arrived([halo])
    act1[0:16] = first_norm(htok[...])
    bgate = dot_nn(act1[...], weights(0, CH))
    xvalue = dot_nn(act1[...], weights(2 * CH, CH))
    xext[...] = (bgate * xvalue).astype(bf16).astype(f32)
    b_s[...] = bgate[16:]
    x_s[...] = xvalue[16:]
    xext[0:16] = jnp.where(seq > 0, xext[0:16], 0.0)
    c_s[...] = dot_nn(act1[16:], weights(CH, CH))
    conv_s[...] = (
        tap0 * xext[14 : ROWS + 14] + tap1 * xext[15 : ROWS + 15] + tap2 * xext[16 : ROWS + 16]
    )
    gated[...] = (c_s[...] * conv_s[...]).astype(bf16)

    def chunk_rows(step):
        return pl.ds(pl.multiple_of(near(y, step) * CHUNK, CHUNK), CHUNK)

    def partial(which, step, values, lo, n):
        for block in range(4):
            part = dot_nt(values, weight_rows(block, lo, n))
            cols = slice(block * 256, block * 256 + 256)
            if step == 0:
                OWN[which, :, cols] = part
            else:
                PY[which, step - 1, :, cols] = part.astype(bf16)
        if step:
            return [send(PY.at[which, step - 1], RY.at[which, step - 1], to_y(step))]
        return []

    def summed(which, copies):
        arrived(copies)
        return (
            OWN[which]
            + RY[which, 0].astype(f32)
            + RY[which, 1].astype(f32)
            + RY[which, 2].astype(f32)
        )

    def ag_y(src, slot):
        return (send(src, slot(y), to_y(1)), send(src, slot(y), to_y(3)))

    def ag_y_pass(copies, slot):
        half = CHUNK // 2
        arrived(copies[:1])
        left = slot(near(y, 3)).at[pl.ds(0, half)]
        out = [send(left, left, to_y(1))]
        arrived(copies[1:])
        right = slot(near(y, 1)).at[pl.ds(half, half)]
        return out + [send(right, right, to_y(3))]

    rs = []
    for step in (2, 1, 3, 0):
        rs += partial(0, step, gated[chunk_rows(step)], OUT0, CH)

    ag1 = ag_three(ag1, GU0, DN0)
    ag2 = ag_three(ag2, DN0, COLS)

    own_rows = chunk_rows(0)
    resid = tok[own_rows] + summed(0, rs)
    res_s[...] = resid
    act2[y] = (resid * rms_scale(resid) * gain_two).astype(bf16)
    def act2_slot(i):
        return act2.at[i]

    ag_act2 = ag_y(act2.at[y], act2_slot)
    arrived(ag1)
    arrived(ag2)

    def ffn_part(acts, ups, rows, f_lo, n):
        gu = dot_nn(acts, weights(GU0 + 2 * f_lo, 2 * n))
        gh = dot_nn(ups, weights(DN0 + f_lo, n))
        for j in range(n // 128):
            gate = gu[:, 256 * j : 256 * j + 128]
            up = gu[:, 256 * j + 128 : 256 * j + 256]
            grad = gh[:, 128 * j : 128 * j + 128]
            sig = jax.nn.sigmoid(gate)
            swish = gate * sig
            hid[rows, pl.ds(f_lo + 128 * j, 128)] = (swish * up).astype(bf16)
            grad_gate = grad * up * sig * (1.0 + gate * (1.0 - sig))
            GG[rows, pl.ds(2 * f_lo + 256 * j, 128)] = grad_gate.astype(bf16)
            GG[rows, pl.ds(2 * f_lo + 256 * j + 128, 128)] = (grad * swish).astype(bf16)

    rs = []
    for step in (0, 1, 3, 2):
        if step == 1:
            ag_act2 = ag_y_pass(ag_act2, act2_slot)
        if step == 2:
            arrived(ag_act2)
        rows = chunk_rows(step)
        acts = act2[near(y, step)]
        ups = ulow[rows]

        @pl.loop(0, 4)
        def _(t):
            ffn_part(acts, ups, rows, pl.multiple_of(t * 256, 256), 256)

        ffn_part(acts, ups, rows, 1024, 128)
        rs += partial(1, step, GG[rows], GU0, 2 * FF)

    def weight_grad(left, right, lo, n):
        for block in range(4):
            values = left(block)
            for start in range(0, n, 384):
                width = min(384, n - start)
                part = dot_tn(values, right[:, pl.ds(start, width)])
                G[block, :, :, :, pl.ds(lo + start, width)] = part.astype(bf16).reshape(
                    4, 2, 32, width
                )

    def rs_core(lo, hi):
        cols = pl.ds(lo, hi - lo)
        return [send(G.at[:, :, oc, :, cols], RC.at[:, :, :, cols], to_core)]

    def rs_one(copies, lo, mid, hi):
        arrived(copies)
        cols = pl.ds(lo, hi - lo)

        @pl.loop(0, 4)
        def _(i):
            for j in range(4):
                G[i, j, c, :, cols] = (
                    G[i, j, c, :, cols].astype(f32) + RC[i, j, :, cols].astype(f32)
                ).astype(bf16)

        a, b = pl.ds(lo, mid - lo), pl.ds(mid, hi - mid)
        out = []
        for s in (1, 3, 2):
            out += [send(G.at[:, near(x, s), c, :, a], RX.at[s - 1, :, :, a], to_x(s))]
            out += [send(G.at[near(z, s), :, c, :, b], RX.at[s - 1, :, :, b], to_z(s))]
        return out

    def rs_two(copies, lo, mid, hi):
        arrived(copies)
        a, b = pl.ds(lo, mid - lo), pl.ds(mid, hi - mid)

        @pl.loop(0, 4)
        def _(i):
            T[i, :, a] = (
                G[i, x, c, :, a].astype(f32)
                + RX[0, i, :, a].astype(f32)
                + RX[1, i, :, a].astype(f32)
                + RX[2, i, :, a].astype(f32)
            ).astype(bf16)
            T[i, :, b] = (
                G[z, i, c, :, b].astype(f32)
                + RX[0, i, :, b].astype(f32)
                + RX[1, i, :, b].astype(f32)
                + RX[2, i, :, b].astype(f32)
            ).astype(bf16)

        out = []
        for s in (1, 3, 2):
            out += [send(T.at[near(z, s), :, a], RZ.at[s - 1, :, a], to_z(s))]
            out += [send(T.at[near(x, s), :, b], RZ.at[s - 1, :, b], to_x(s))]
        return out

    def rs_end(lo, n, mid):
        cols = pl.ds(lo, n)
        mine = z if lo < mid else x
        return (
            T[mine, :, cols].astype(f32)
            + RZ[0, :, cols].astype(f32)
            + RZ[1, :, cols].astype(f32)
            + RZ[2, :, cols].astype(f32)
        )

    gi = (IN0, 512, SM0)
    weight_grad(
        lambda i: act2[:, :, i * 256 : i * 256 + 256].reshape(ROWS, 256), GG, GU0, 2 * FF
    )
    r_gu = rs_core(GU0, DN0)

    back_two = summed(1, rs)
    resid = res_s[...]
    scale_two = rms_scale(resid)
    normed = resid * scale_two
    SM[0] = jnp.zeros((8, D), f32)
    SM[0, 4:5] = jnp.sum(back_two * normed, axis=0, keepdims=True)
    scaled = back_two * gain_two
    grad_resid = cot[own_rows] + scale_two * (
        scaled - normed * jnp.mean(scaled * normed, axis=-1, keepdims=True)
    )
    rlow[y] = grad_resid.astype(bf16)

    def rlow_slot(i):
        return rlow.at[i]

    ag_rlow = ag_y(rlow.at[y], rlow_slot)
    OWN[1] = grad_resid

    weight_grad(lambda i: ulow[:, i * 256 : i * 256 + 256], hid, DN0, FF)
    r_dn = rs_core(DN0, COLS)
    rs_ffn = partial(2, 2, hid[chunk_rows(2)], DN0, FF)
    r_gu = rs_one(r_gu, *g1)
    ag_rlow = ag_y_pass(ag_rlow, rlow_slot)
    for step in (1, 3, 0):
        rs_ffn += partial(2, step, hid[chunk_rows(step)], DN0, FF)
    r_dn = rs_one(r_dn, *g2)

    arrived(ag_rlow)
    low = rlow[...].reshape(ROWS, D)
    grad_gated = dot_nn(low, weights(OUT0, CH))
    gext[0:ROWS] = (grad_gated * c_s[...]).astype(bf16).astype(f32)
    mxb[...] = gext[0:16].astype(bf16)
    halo = send(mxb, hb, to_prev)
    GB[:, CH : 2 * CH] = (grad_gated * conv_s[...]).astype(bf16)
    grad_conv = gext[0:ROWS]
    for k in range(3):
        row = jnp.sum(grad_conv * xext[14 + k : ROWS + 14 + k], axis=0, keepdims=True)
        SM[0, k : k + 1, own_channels] = row
    weight_grad(
        lambda i: rlow[:, :, i * 256 : i * 256 + 256].reshape(ROWS, 256), gated, OUT0, CH
    )
    arrived([halo])
    gext[ROWS : ROWS + 8] = jnp.where(seq < 7, hb[...].astype(f32)[0:8], 0.0)
    grad_mixed = tap2 * gext[0:ROWS] + tap1 * gext[1 : ROWS + 1] + tap0 * gext[2 : ROWS + 2]
    GB[:, 0:CH] = (grad_mixed * x_s[...]).astype(bf16)
    GB[:, 2 * CH : 3 * CH] = (grad_mixed * b_s[...]).astype(bf16)

    rs = []
    for step in (2, 1, 3, 0):
        rs += partial(3, step, GB[chunk_rows(step)], IN0, 3 * CH)

    weight_grad(lambda i: act1[16:, i * 256 : i * 256 + 256], GB, IN0, 3 * CH)
    r_in = rs_core(IN0, SM0)
    r_gu = rs_two(r_gu, *g1)
    r_dn = rs_two(r_dn, *g2)

    mixrow[...] = (res_s[...] + summed(2, rs_ffn)).astype(bf16)

    def mixed_slot(i):
        return mixed_o.at[i]

    ag_mixed = ag_y(mixrow, mixed_slot)
    local_mixed = pltpu.make_async_copy(mixrow, mixed_o.at[y], lsem.at[0])
    local_mixed.start()
    r_in = rs_one(r_in, *gi)

    back_one = summed(3, rs)
    own_tok = tok[own_rows]
    scale_one = rms_scale(own_tok)
    normed = own_tok * scale_one
    SM[0, 3:4] = jnp.sum(back_one * normed, axis=0, keepdims=True)
    scaled = back_one * gain_one
    tgrow[...] = (
        OWN[1]
        + scale_one * (scaled - normed * jnp.mean(scaled * normed, axis=-1, keepdims=True))
    ).astype(bf16)

    def tg_slot(i):
        return tg_o.at[i]

    ag_tg = ag_y(tgrow, tg_slot)
    local_tg = pltpu.make_async_copy(tgrow, tg_o.at[y], lsem.at[1])
    local_tg.start()

    sm = [send(SM.at[0], SMR.at[0], to_core)]
    ag_mixed = ag_y_pass(ag_mixed, mixed_slot)
    arrived(sm)
    SM[1] = SM[0] + SMR[0]
    sm = [send(SM.at[1], SMR.at[s], to_x(s)) for s in (1, 3, 2)]

    arrived(r_dn)
    g_dn[:, 0:640] = rs_end(DN0, 640, g2[1])
    g_dn[:, 640:1152] = rs_end(DN0 + 640, 512, g2[1])

    r_in = rs_two(r_in, *gi)
    arrived(sm)
    SM[2] = SM[1] + SMR[1] + SMR[2] + SMR[3]
    sm = [send(SM.at[2], SMR.at[3 + s], to_z(s)) for s in (1, 3, 2)]

    ag_tg = ag_y_pass(ag_tg, tg_slot)
    arrived(r_gu)
    for t in range(9):
        g_gu[0, :, 128 * t : 128 * t + 128] = rs_end(GU0 + 256 * t, 128, g1[1])
        g_gu[1, :, 128 * t : 128 * t + 128] = rs_end(GU0 + 256 * t + 128, 128, g1[1])

    arrived(sm)
    SMR[7] = SM[2] + SMR[4] + SMR[5] + SMR[6]
    sm = [send(SMR.at[7], SMR.at[7 + s], to_y(s)) for s in (1, 3, 2)]

    arrived(r_in)
    for k in range(3):
        g_in[k] = rs_end(IN0 + CH * k, CH, gi[1])
    g_out[...] = rs_end(OUT0, CH, gi[1])

    arrived(sm)

    def term(j):
        return SMR[7 + lax.rem(y - j + 4, 4)]

    small_o[...] = ((term(0) + term(1)) + term(2)) + term(3)

    arrived(ag_mixed)
    arrived(ag_tg)
    local_mixed.wait()
    local_tg.wait()
    for copy in pending:
        copy.wait_send()


def local(
    tokens,
    cotangent,
    in_weight,
    in_first,
    in_second,
    out_weight,
    out_first,
    out_second,
    gu_weight,
    gu_first,
    gu_second,
    down_weight,
    down_first,
    down_second,
    conv_weight,
    conv_first,
    conv_second,
    norm_gains,
    gains_first,
    gains_second,
):
    vmem = pl.BlockSpec(memory_space=pltpu.VMEM)
    hbm = pl.BlockSpec(memory_space=pl.ANY)
    shape = jax.ShapeDtypeStruct
    mixed, tg, grad_in, grad_out, grad_gu, grad_dn, grad_small = pl.pallas_call(
        kernel,
        out_shape=(
            shape((4, CHUNK, D), bf16),
            shape((4, CHUNK, D), bf16),
            shape((3, 32, CH), f32),
            shape((32, CH), f32),
            shape((2, 32, FF), f32),
            shape((32, FF), f32),
            shape((8, D), f32),
        ),
        in_specs=[hbm] * 2 + [vmem] * 6,
        out_specs=(hbm, hbm, vmem, vmem, vmem, vmem, vmem),
        scratch_shapes=[
            pltpu.VMEM((ROWS, D), f32),
            pltpu.VMEM((ROWS, D), f32),
            pltpu.VMEM((16, D), f32),
            pltpu.VMEM((128, 128), f32),
            pltpu.VMEM((4, 4, 2, 32, COLS), bf16),
            pltpu.VMEM((4, 4, 2, 32, COLS), bf16),
            pltpu.VMEM((4, 4, 32, COLS), bf16),
            pltpu.VMEM((3, 4, 32, COLS), bf16),
            pltpu.VMEM((4, 32, COLS), bf16),
            pltpu.VMEM((3, 32, COLS), bf16),
            pltpu.VMEM((ROWS + 16, D), bf16),
            pltpu.VMEM((ROWS, D), bf16),
            pltpu.VMEM((4, CHUNK, D), bf16),
            pltpu.VMEM((4, CHUNK, D), bf16),
            pltpu.VMEM((ROWS, FF), bf16),
            pltpu.VMEM((ROWS, 2 * FF), bf16),
            pltpu.VMEM((ROWS, CH), f32),
            pltpu.VMEM((ROWS, CH), f32),
            pltpu.VMEM((ROWS, CH), f32),
            pltpu.VMEM((ROWS, CH), f32),
            pltpu.VMEM((ROWS + 16, CH), f32),
            pltpu.VMEM((ROWS + 8, CH), f32),
            pltpu.VMEM((16, CH), bf16),
            pltpu.VMEM((ROWS, CH), bf16),
            pltpu.VMEM((ROWS, 3 * CH), bf16),
            pltpu.VMEM((16, CH), bf16),
            pltpu.VMEM((8, D), f32),
            pltpu.VMEM((3, 8, D), f32),
            pltpu.VMEM((11, 8, D), f32),
            pltpu.VMEM((4, 3, CHUNK, D), bf16),
            pltpu.VMEM((4, 3, CHUNK, D), bf16),
            pltpu.VMEM((4, CHUNK, D), f32),
            pltpu.VMEM((CHUNK, D), f32),
            pltpu.VMEM((CHUNK, D), bf16),
            pltpu.VMEM((CHUNK, D), bf16),
            pltpu.SemaphoreType.DMA((N_SEMS,)),
            pltpu.SemaphoreType.DMA((N_SEMS,)),
            pltpu.SemaphoreType.DMA((4,)),
        ],
        name="block_step",
        compiler_params=pltpu.CompilerParams(
            collective_id=0, has_side_effects=True, vmem_limit_bytes=62 << 20
        ),
    )(
        tokens.reshape(ROWS, D),
        cotangent.reshape(ROWS, D),
        in_weight,
        out_weight,
        gu_weight,
        down_weight,
        conv_weight,
        norm_gains,
    )
    here = (lax.axis_index("dp") * 8 + lax.axis_index("seq")) * 32
    conv_grad = lax.dynamic_slice(grad_small, (0, here), (3, 32))
    gains_grad = lax.dynamic_slice(grad_small, (3, here), (2, 32))
    in_new = adamw(in_weight, in_first, in_second, grad_in, rate_matrix, decay_matrix)
    out_new = adamw(out_weight, out_first, out_second, grad_out.T, rate_matrix, decay_matrix)
    gu_new = adamw(gu_weight, gu_first, gu_second, grad_gu, rate_matrix, decay_matrix)
    down_new = adamw(down_weight, down_first, down_second, grad_dn.T, rate_matrix, decay_matrix)
    conv_new = adamw(conv_weight, conv_first, conv_second, conv_grad, rate_small, 0.0)
    gains_new = adamw(norm_gains, gains_first, gains_second, gains_grad, rate_small, 0.0)
    return (
        mixed.reshape(tokens.shape).astype(f32),
        tg.reshape(tokens.shape).astype(f32),
        *in_new,
        *out_new,
        *gu_new,
        *down_new,
        *conv_new,
        *gains_new,
    )


def solution(mesh):
    rows = P("dp", "seq", None)
    stack = P(None, ("dp", "seq"), "mp")
    flat = P("mp", ("dp", "seq"))
    thin = P(None, ("dp", "seq"))
    groups = (stack,) * 3 + (flat,) * 3 + (stack,) * 3 + (flat,) * 3 + (thin,) * 6
    return jax.shard_map(
        local,
        mesh=mesh,
        in_specs=(rows, rows) + groups,
        out_specs=(rows, rows) + groups,
        check_vma=False,
    )
```

```python
import jax
import jax.numpy as jnp
from jax import lax
from jax.experimental import pallas as pl
from jax.experimental.pallas import tpu as pltpu
from jax.sharding import PartitionSpec as P

STEP = 10

beta_one = 0.9
beta_two = 0.95
eps_adam = 1e-08
eps_norm = 1e-05
rate_matrix = 0.05
rate_small = 0.3
decay_matrix = 0.1

MESH = pl.DeviceIdType.MESH
bf16 = jnp.bfloat16
f32 = jnp.float32

ROWS = 512
CHUNK = 128
D = 1024
CH = 256
FF = 1152
IN0, OUT0, SM0, GU0, DN0, COLS = 0, 768, 1024, 1152, 3456, 4608


def adamw(master, first, second, grad, rate, decay):
    moment = beta_one * first + (1.0 - beta_one) * grad
    square = beta_two * second + (1.0 - beta_two) * grad * grad
    moment_hat = moment / (1.0 - beta_one**STEP)
    square_hat = square / (1.0 - beta_two**STEP)
    renewed = master - rate * (moment_hat / (jnp.sqrt(square_hat) + eps_adam) + decay * master)
    return (renewed, moment, square)


def rms_scale(values):
    return lax.rsqrt(jnp.mean(values * values, axis=-1, keepdims=True) + eps_norm)


def dot_nn(a, b):
    return jnp.dot(a, b, preferred_element_type=f32)


def dot_nt(a, b):
    return lax.dot_general(a, b, (((1,), (1,)), ((), ())), preferred_element_type=f32)


def dot_tn(a, b):
    return lax.dot_general(a, b, (((0,), (0,)), ((), ())), preferred_element_type=f32)


N_SEMS = 144


def kernel(
    tok_h,
    cot_h,
    w_in,
    w_out,
    w_gu,
    w_dn,
    w_conv,
    w_gain,
    mixed_o,
    tg_o,
    g_in,
    g_out,
    g_gu,
    g_dn,
    small_o,
    tok,
    cot,
    htok,
    square,
    W,
    G,
    RC,
    RX,
    T,
    RZ,
    act1,
    ulow,
    act2,
    rlow,
    hid,
    GG,
    b_s,
    c_s,
    x_s,
    conv_s,
    xext,
    gext,
    mxb,
    gated,
    GB,
    hb,
    smw,
    SM,
    SMR,
    PY,
    RY,
    OWN,
    res_s,
    mixrow,
    tgrow,
    ssem,
    rsem,
    lsem,
):
    z = lax.axis_index("dp")
    seq = lax.axis_index("seq")
    y = lax.axis_index("mp")
    x = seq // 2
    c = lax.rem(seq, 2)
    oc = 1 - c

    def near(value, step):
        return lax.rem(value + step, 4)

    def to_x(step):
        return (z, near(x, step) * 2 + c, y)

    def to_z(step):
        return (near(z, step), seq, y)

    def to_y(step):
        return (z, seq, near(y, step))

    to_core = (z, x * 2 + oc, y)
    to_next = (z, lax.rem(seq + 1, 8), y)
    to_prev = (z, lax.rem(seq + 7, 8), y)

    counter = [0]
    pending = []

    def send(src, dst, where):
        i = counter[0]
        assert i < N_SEMS
        counter[0] += 1
        copy = pltpu.make_async_remote_copy(
            src, dst, ssem.at[i], rsem.at[i], device_id=where, device_id_type=MESH
        )
        copy.start()
        pending.append(copy)
        return copy

    def arrived(copies):
        for copy in copies:
            copy.wait_recv()

    barrier = pltpu.get_barrier_semaphore()
    peers = [to_core, to_next, to_prev]
    for step in (1, 2, 3):
        peers += [to_x(step), to_z(step), to_y(step)]
    for peer in peers:
        pl.semaphore_signal(barrier, inc=1, device_id=peer, device_id_type=MESH)
    load_tok = pltpu.make_async_copy(tok_h, tok, lsem.at[2])
    load_tok.start()
    load_cot = pltpu.make_async_copy(cot_h, cot, lsem.at[3])
    load_cot.start()

    for k in range(3):
        W[z, x, c, :, CH * k : CH * k + CH] = w_in[k].astype(bf16)
    W[z, x, c, :, OUT0:SM0] = w_out[...].astype(bf16)
    square[...] = jnp.zeros((128, 128), f32)
    square[0:3, 0:32] = w_conv[...]
    square[3:5, 0:32] = w_gain[...]
    W[z, x, c, :, SM0:GU0] = square[...].T[0:32].astype(bf16)
    for t in range(9):
        for k in range(2):
            at = GU0 + 256 * t + 128 * k
            W[z, x, c, :, at : at + 128] = w_gu[k, :, 128 * t : 128 * t + 128].astype(bf16)
    W[z, x, c, :, DN0:COLS] = w_dn[...].astype(bf16)
    pl.semaphore_wait(barrier, len(peers))

    def ag_one(lo, mid, hi):
        a, b = pl.ds(lo, mid - lo), pl.ds(mid, hi - mid)
        src_a, src_b = W.at[z, x, c, :, a], W.at[z, x, c, :, b]
        return (
            [send(src_a, src_a, to_x(s)) for s in (1, 3, 2)],
            [send(src_b, src_b, to_z(s)) for s in (1, 3, 2)],
        )

    def ag_two(copies, lo, mid, hi):
        a, b = pl.ds(lo, mid - lo), pl.ds(mid, hi - mid)
        src_a, src_b = W.at[z, :, c, :, a], W.at[:, x, c, :, b]
        arrived(copies[0])
        first = [send(src_a, src_a, to_z(s)) for s in (1, 3)]
        arrived(copies[1])
        return first, [send(src_b, src_b, to_x(s)) for s in (1, 3)]

    def ag_pass(copies, lo, mid, hi):
        a, b = pl.ds(lo, mid - lo), pl.ds(mid, hi - mid)
        low, high = pl.ds(0, 2), pl.ds(2, 2)
        out = []
        for s, half in ((1, low), (3, high)):
            i = 0 if s == 1 else 1
            arrived([copies[0][i]])
            src = W.at[near(z, 4 - s), half, c, :, a]
            out += [send(src, src, to_z(s))]
            arrived([copies[1][i]])
            src = W.at[half, near(x, 4 - s), c, :, b]
            out += [send(src, src, to_x(s))]
        return out

    def ag_three(copies, lo, hi):
        arrived(copies)
        src = W.at[:, :, c, :, pl.ds(lo, hi - lo)]
        return [send(src, src, to_core)]

    g0 = (IN0, 640, GU0)
    g1 = (GU0, GU0 + 1152, DN0)
    g2 = (DN0, DN0 + 640, COLS)
    ag0 = ag_one(*g0)
    halo = send(tok_h.at[pl.ds(ROWS - 16, 16)], htok, to_next)
    load_cot.wait()
    for r in range(0, ROWS, 128):
        ulow[r : r + 128] = cot[r : r + 128].astype(bf16)
    ag0 = ag_two(ag0, *g0)
    ag1 = ag_one(*g1)
    ag2 = ag_one(*g2)
    ag0 = ag_pass(ag0, *g0)
    ag1 = ag_two(ag1, *g1)
    ag0 = ag_three(ag0, IN0, GU0)
    ag2 = ag_two(ag2, *g2)
    arrived(ag0)

    def weights(lo, n):
        return W[:, :, :, :, pl.ds(lo, n)].reshape(D, n)

    def weight_rows(block, lo, n):
        return W[block, :, :, :, pl.ds(lo, n)].reshape(256, n)

    smw[...] = weights(SM0, 128).astype(f32).T[:8]
    gain_one = smw[3:4]
    gain_two = smw[4:5]
    own_channels = pl.ds(pl.multiple_of(y * CH, CH), CH)
    taps = smw[:, own_channels]
    tap0, tap1, tap2 = taps[0:1], taps[1:2], taps[2:3]

    def first_norm(v):
        return (v * rms_scale(v) * gain_one).astype(bf16)

    load_tok.wait()
    for r in range(0, ROWS, 128):
        act1[r + 16 : r + 144] = first_norm(tok[r : r + 128])
    arrived([halo])
    act1[0:16] = first_norm(htok[...])
    bgate = dot_nn(act1[...], weights(0, CH))
    xvalue = dot_nn(act1[...], weights(2 * CH, CH))
    xext[...] = (bgate * xvalue).astype(bf16).astype(f32)
    b_s[...] = bgate[16:]
    x_s[...] = xvalue[16:]
    xext[0:16] = jnp.where(seq > 0, xext[0:16], 0.0)
    c_s[...] = dot_nn(act1[16:], weights(CH, CH))
    conv_s[...] = (
        tap0 * xext[14 : ROWS + 14] + tap1 * xext[15 : ROWS + 15] + tap2 * xext[16 : ROWS + 16]
    )
    gated[...] = (c_s[...] * conv_s[...]).astype(bf16)

    def chunk_rows(step):
        return pl.ds(pl.multiple_of(near(y, step) * CHUNK, CHUNK), CHUNK)

    def partial(which, step, values, lo, n):
        for block in range(4):
            part = dot_nt(values, weight_rows(block, lo, n))
            cols = slice(block * 256, block * 256 + 256)
            if step == 0:
                OWN[which, :, cols] = part
            else:
                PY[which, step - 1, :, cols] = part.astype(bf16)
        if step:
            return [send(PY.at[which, step - 1], RY.at[which, step - 1], to_y(step))]
        return []

    half = CHUNK // 2
    low_half, high_half = pl.ds(0, half), pl.ds(half, half)

    def part_of(which, slot, rows, where):
        return send(PY.at[which, slot, rows], RY.at[which, slot, rows], where)

    def rs_y(which, source, lo, n):
        def block_of(step):
            return source[chunk_rows(step)]

        for step in (2, 1, 3, 0):
            values = block_of(step)
            for block in range(4):
                part = dot_nt(values, weight_rows(block, lo, n))
                cols = slice(block * 256, block * 256 + 256)
                if step == 0:
                    OWN[which, :, cols] = part
                else:
                    PY[which, step - 1, :, cols] = part.astype(bf16)
            if step == 2:
                relay = (
                    part_of(which, 1, low_half, to_y(1)),
                    part_of(which, 1, high_half, to_y(3)),
                )
            elif step == 1:
                direct = [part_of(which, 0, high_half, to_y(1))]
            elif step == 3:
                direct += [part_of(which, 2, low_half, to_y(3))]
        return relay, direct

    def rs_y_pass(which, state):
        relay, direct = state
        out = list(direct)
        for k, (slot, rows, where) in enumerate(
            ((0, slice(0, half), to_y(1)), (2, slice(half, CHUNK), to_y(3)))
        ):
            arrived([relay[k]])
            PY[which, slot, rows] = (
                PY[which, slot, rows].astype(f32) + RY[which, 1, rows].astype(f32)
            ).astype(bf16)
            out += [part_of(which, slot, low_half if k == 0 else high_half, where)]
        return out

    def summed_relayed(which, copies):
        arrived(copies)
        return OWN[which] + RY[which, 0].astype(f32) + RY[which, 2].astype(f32)

    def summed(which, copies):
        arrived(copies)
        return (
            OWN[which]
            + RY[which, 0].astype(f32)
            + RY[which, 1].astype(f32)
            + RY[which, 2].astype(f32)
        )

    def ag_y(src, slot):
        return (send(src, slot(y), to_y(1)), send(src, slot(y), to_y(3)))

    def ag_y_pass(copies, slot):
        arrived(copies[:1])
        left = slot(near(y, 3)).at[pl.ds(0, half)]
        out = [send(left, left, to_y(1))]
        arrived(copies[1:])
        right = slot(near(y, 1)).at[pl.ds(half, half)]
        return out + [send(right, right, to_y(3))]

    rs = rs_y(0, gated, OUT0, CH)
    ag1 = ag_pass(ag1, *g1)
    rs = rs_y_pass(0, rs)
    ag2 = ag_pass(ag2, *g2)
    ag1 = ag_three(ag1, GU0, DN0)
    ag2 = ag_three(ag2, DN0, COLS)

    own_rows = chunk_rows(0)
    resid = tok[own_rows] + summed_relayed(0, rs)
    res_s[...] = resid
    act2[y] = (resid * rms_scale(resid) * gain_two).astype(bf16)
    def act2_slot(i):
        return act2.at[i]

    ag_act2 = ag_y(act2.at[y], act2_slot)
    arrived(ag1)
    arrived(ag2)

    def ffn_part(acts, ups, rows, f_lo, n):
        gu = dot_nn(acts, weights(GU0 + 2 * f_lo, 2 * n))
        gh = dot_nn(ups, weights(DN0 + f_lo, n))
        for j in range(n // 128):
            gate = gu[:, 256 * j : 256 * j + 128]
            up = gu[:, 256 * j + 128 : 256 * j + 256]
            grad = gh[:, 128 * j : 128 * j + 128]
            sig = jax.nn.sigmoid(gate)
            swish = gate * sig
            hid[rows, pl.ds(f_lo + 128 * j, 128)] = (swish * up).astype(bf16)
            grad_gate = grad * up * sig * (1.0 + gate * (1.0 - sig))
            GG[rows, pl.ds(2 * f_lo + 256 * j, 128)] = grad_gate.astype(bf16)
            GG[rows, pl.ds(2 * f_lo + 256 * j + 128, 128)] = (grad * swish).astype(bf16)

    rs = []
    for step in (0, 1, 3, 2):
        if step == 1:
            ag_act2 = ag_y_pass(ag_act2, act2_slot)
        if step == 2:
            arrived(ag_act2)
        rows = chunk_rows(step)
        acts = act2[near(y, step)]
        ups = ulow[rows]

        @pl.loop(0, 4)
        def _(t):
            ffn_part(acts, ups, rows, pl.multiple_of(t * 256, 256), 256)

        ffn_part(acts, ups, rows, 1024, 128)
        rs += partial(1, step, GG[rows], GU0, 2 * FF)

    def weight_grad(left, right, lo, n):
        for block in range(4):
            values = left(block)
            for start in range(0, n, 384):
                width = min(384, n - start)
                part = dot_tn(values, right[:, pl.ds(start, width)])
                G[block, :, :, :, pl.ds(lo + start, width)] = part.astype(bf16).reshape(
                    4, 2, 32, width
                )

    def rs_core(lo, hi):
        cols = pl.ds(lo, hi - lo)
        return [send(G.at[:, :, oc, :, cols], RC.at[:, :, :, cols], to_core)]

    def rs_one(copies, lo, mid, hi):
        arrived(copies)
        cols = pl.ds(lo, hi - lo)

        @pl.loop(0, 4)
        def _(i):
            for j in range(4):
                G[i, j, c, :, cols] = (
                    G[i, j, c, :, cols].astype(f32) + RC[i, j, :, cols].astype(f32)
                ).astype(bf16)

        a, b = pl.ds(lo, mid - lo), pl.ds(mid, hi - mid)
        out = []
        for s in (1, 3, 2):
            out += [send(G.at[:, near(x, s), c, :, a], RX.at[s - 1, :, :, a], to_x(s))]
            out += [send(G.at[near(z, s), :, c, :, b], RX.at[s - 1, :, :, b], to_z(s))]
        return out

    def rs_two(copies, lo, mid, hi):
        arrived(copies)
        a, b = pl.ds(lo, mid - lo), pl.ds(mid, hi - mid)

        @pl.loop(0, 4)
        def _(i):
            T[i, :, a] = (
                G[i, x, c, :, a].astype(f32)
                + RX[0, i, :, a].astype(f32)
                + RX[1, i, :, a].astype(f32)
                + RX[2, i, :, a].astype(f32)
            ).astype(bf16)
            T[i, :, b] = (
                G[z, i, c, :, b].astype(f32)
                + RX[0, i, :, b].astype(f32)
                + RX[1, i, :, b].astype(f32)
                + RX[2, i, :, b].astype(f32)
            ).astype(bf16)

        out = []
        for s in (1, 3, 2):
            out += [send(T.at[near(z, s), :, a], RZ.at[s - 1, :, a], to_z(s))]
            out += [send(T.at[near(x, s), :, b], RZ.at[s - 1, :, b], to_x(s))]
        return out

    def rs_end(lo, n, mid):
        cols = pl.ds(lo, n)
        mine = z if lo < mid else x
        return (
            T[mine, :, cols].astype(f32)
            + RZ[0, :, cols].astype(f32)
            + RZ[1, :, cols].astype(f32)
            + RZ[2, :, cols].astype(f32)
        )

    gi = (IN0, 512, SM0)
    gi = (IN0, 512, SM0)
    rs_ffn = rs_y(2, hid, DN0, FF)

    back_two = summed(1, rs)
    resid = res_s[...]
    scale_two = rms_scale(resid)
    normed = resid * scale_two
    SM[0] = jnp.zeros((8, D), f32)
    SM[0, 4:5] = jnp.sum(back_two * normed, axis=0, keepdims=True)
    scaled = back_two * gain_two
    grad_resid = cot[own_rows] + scale_two * (
        scaled - normed * jnp.mean(scaled * normed, axis=-1, keepdims=True)
    )
    rlow[y] = grad_resid.astype(bf16)

    def rlow_slot(i):
        return rlow.at[i]

    ag_rlow = ag_y(rlow.at[y], rlow_slot)
    OWN[1] = grad_resid

    weight_grad(
        lambda i: act2[:, :, i * 256 : i * 256 + 256].reshape(ROWS, 256), GG, GU0, 2 * FF
    )
    r_gu = rs_core(GU0, DN0)
    ag_rlow = ag_y_pass(ag_rlow, rlow_slot)
    rs_ffn = rs_y_pass(2, rs_ffn)
    weight_grad(lambda i: ulow[:, i * 256 : i * 256 + 256], hid, DN0, FF)
    r_dn = rs_core(DN0, COLS)
    r_gu = rs_one(r_gu, *g1)

    arrived(ag_rlow)
    low = rlow[...].reshape(ROWS, D)
    grad_gated = dot_nn(low, weights(OUT0, CH))
    gext[0:ROWS] = (grad_gated * c_s[...]).astype(bf16).astype(f32)
    mxb[...] = gext[0:16].astype(bf16)
    halo = send(mxb, hb, to_prev)
    GB[:, CH : 2 * CH] = (grad_gated * conv_s[...]).astype(bf16)
    grad_conv = gext[0:ROWS]
    for k in range(3):
        row = jnp.sum(grad_conv * xext[14 + k : ROWS + 14 + k], axis=0, keepdims=True)
        SM[0, k : k + 1, own_channels] = row
    weight_grad(
        lambda i: rlow[:, :, i * 256 : i * 256 + 256].reshape(ROWS, 256), gated, OUT0, CH
    )
    arrived([halo])
    gext[ROWS : ROWS + 8] = jnp.where(seq < 7, hb[...].astype(f32)[0:8], 0.0)
    grad_mixed = tap2 * gext[0:ROWS] + tap1 * gext[1 : ROWS + 1] + tap0 * gext[2 : ROWS + 2]
    GB[:, 0:CH] = (grad_mixed * x_s[...]).astype(bf16)
    GB[:, 2 * CH : 3 * CH] = (grad_mixed * b_s[...]).astype(bf16)

    rs = rs_y(3, GB, IN0, 3 * CH)
    weight_grad(lambda i: act1[16:, i * 256 : i * 256 + 256], GB, IN0, 3 * CH)
    r_in = rs_core(IN0, SM0)
    r_dn = rs_one(r_dn, *g2)
    rs = rs_y_pass(3, rs)

    mixrow[...] = (res_s[...] + summed_relayed(2, rs_ffn)).astype(bf16)

    def mixed_slot(i):
        return mixed_o.at[i]

    ag_mixed = ag_y(mixrow, mixed_slot)
    local_mixed = pltpu.make_async_copy(mixrow, mixed_o.at[y], lsem.at[0])
    local_mixed.start()
    r_gu = rs_two(r_gu, *g1)
    r_in = rs_one(r_in, *gi)

    back_one = summed_relayed(3, rs)
    own_tok = tok[own_rows]
    scale_one = rms_scale(own_tok)
    normed = own_tok * scale_one
    SM[0, 3:4] = jnp.sum(back_one * normed, axis=0, keepdims=True)
    scaled = back_one * gain_one
    tgrow[...] = (
        OWN[1]
        + scale_one * (scaled - normed * jnp.mean(scaled * normed, axis=-1, keepdims=True))
    ).astype(bf16)

    def tg_slot(i):
        return tg_o.at[i]

    ag_tg = ag_y(tgrow, tg_slot)
    local_tg = pltpu.make_async_copy(tgrow, tg_o.at[y], lsem.at[1])
    local_tg.start()

    sm = [send(SM.at[0], SMR.at[0], to_core)]
    ag_mixed = ag_y_pass(ag_mixed, mixed_slot)
    r_dn = rs_two(r_dn, *g2)
    arrived(sm)
    SM[1] = SM[0] + SMR[0]
    sm = [send(SM.at[1], SMR.at[s], to_x(s)) for s in (1, 3, 2)]

    arrived(r_dn)
    g_dn[:, 0:640] = rs_end(DN0, 640, g2[1])
    g_dn[:, 640:1152] = rs_end(DN0 + 640, 512, g2[1])

    r_in = rs_two(r_in, *gi)
    arrived(sm)
    SM[2] = SM[1] + SMR[1] + SMR[2] + SMR[3]
    sm = [send(SM.at[2], SMR.at[3 + s], to_z(s)) for s in (1, 3, 2)]

    ag_tg = ag_y_pass(ag_tg, tg_slot)
    arrived(r_gu)
    for t in range(9):
        g_gu[0, :, 128 * t : 128 * t + 128] = rs_end(GU0 + 256 * t, 128, g1[1])
        g_gu[1, :, 128 * t : 128 * t + 128] = rs_end(GU0 + 256 * t + 128, 128, g1[1])

    arrived(sm)
    SMR[7] = SM[2] + SMR[4] + SMR[5] + SMR[6]
    sm = [send(SMR.at[7], SMR.at[7 + s], to_y(s)) for s in (1, 3, 2)]

    arrived(r_in)
    for k in range(3):
        g_in[k] = rs_end(IN0 + CH * k, CH, gi[1])
    g_out[...] = rs_end(OUT0, CH, gi[1])

    arrived(sm)

    def term(j):
        return SMR[7 + lax.rem(y - j + 4, 4)]

    shard_at = z * 8 + seq
    SMR[0] = ((term(0) + term(1)) + term(2)) + term(3)
    four = SMR[0, :, pl.ds(pl.multiple_of(shard_at // 4 * 128, 128), 128)]
    place = lax.rem(shard_at, 4)
    mine = four[:, 0:32]
    for k in range(1, 4):
        mine = jnp.where(place == k, four[:, 32 * k : 32 * k + 32], mine)
    small_o[...] = mine

    arrived(ag_mixed)
    arrived(ag_tg)
    local_mixed.wait()
    local_tg.wait()
    for copy in pending:
        copy.wait_send()


def finish(*refs):
    refs[25][...] = refs[0][...].astype(f32)
    refs[26][...] = refs[1][...].astype(f32)
    small = refs[6][...]
    grads = [ref[...] for ref in refs[2:6]] + [small[0:3], small[3:5]]
    for k, grad in enumerate(grads):
        rate, decay = (rate_matrix, decay_matrix) if k < 4 else (rate_small, 0.0)
        group = refs[7 + 3 * k : 10 + 3 * k]
        new = adamw(*(ref[...] for ref in group), grad, rate, decay)
        for ref, value in zip(refs[27 + 3 * k : 30 + 3 * k], new):
            ref[...] = value


def local(
    tokens,
    cotangent,
    in_weight,
    in_first,
    in_second,
    out_weight,
    out_first,
    out_second,
    gu_weight,
    gu_first,
    gu_second,
    down_weight,
    down_first,
    down_second,
    conv_weight,
    conv_first,
    conv_second,
    norm_gains,
    gains_first,
    gains_second,
):
    vmem = pl.BlockSpec(memory_space=pltpu.VMEM)
    hbm = pl.BlockSpec(memory_space=pl.ANY)
    shape = jax.ShapeDtypeStruct
    mixed, tg, grad_in, grad_out, grad_gu, grad_dn, grad_small = pl.pallas_call(
        kernel,
        out_shape=(
            shape((4, CHUNK, D), bf16),
            shape((4, CHUNK, D), bf16),
            shape((3, 32, CH), f32),
            shape((32, CH), f32),
            shape((2, 32, FF), f32),
            shape((32, FF), f32),
            shape((8, 32), f32),
        ),
        in_specs=[hbm] * 2 + [vmem] * 6,
        out_specs=(hbm, hbm, vmem, vmem, vmem, vmem, vmem),
        scratch_shapes=[
            pltpu.VMEM((ROWS, D), f32),
            pltpu.VMEM((ROWS, D), f32),
            pltpu.VMEM((16, D), f32),
            pltpu.VMEM((128, 128), f32),
            pltpu.VMEM((4, 4, 2, 32, COLS), bf16),
            pltpu.VMEM((4, 4, 2, 32, COLS), bf16),
            pltpu.VMEM((4, 4, 32, COLS), bf16),
            pltpu.VMEM((3, 4, 32, COLS), bf16),
            pltpu.VMEM((4, 32, COLS), bf16),
            pltpu.VMEM((3, 32, COLS), bf16),
            pltpu.VMEM((ROWS + 16, D), bf16),
            pltpu.VMEM((ROWS, D), bf16),
            pltpu.VMEM((4, CHUNK, D), bf16),
            pltpu.VMEM((4, CHUNK, D), bf16),
            pltpu.VMEM((ROWS, FF), bf16),
            pltpu.VMEM((ROWS, 2 * FF), bf16),
            pltpu.VMEM((ROWS, CH), f32),
            pltpu.VMEM((ROWS, CH), f32),
            pltpu.VMEM((ROWS, CH), f32),
            pltpu.VMEM((ROWS, CH), f32),
            pltpu.VMEM((ROWS + 16, CH), f32),
            pltpu.VMEM((ROWS + 8, CH), f32),
            pltpu.VMEM((16, CH), bf16),
            pltpu.VMEM((ROWS, CH), bf16),
            pltpu.VMEM((ROWS, 3 * CH), bf16),
            pltpu.VMEM((16, CH), bf16),
            pltpu.VMEM((8, D), f32),
            pltpu.VMEM((3, 8, D), f32),
            pltpu.VMEM((11, 8, D), f32),
            pltpu.VMEM((4, 3, CHUNK, D), bf16),
            pltpu.VMEM((4, 3, CHUNK, D), bf16),
            pltpu.VMEM((4, CHUNK, D), f32),
            pltpu.VMEM((CHUNK, D), f32),
            pltpu.VMEM((CHUNK, D), bf16),
            pltpu.VMEM((CHUNK, D), bf16),
            pltpu.SemaphoreType.DMA((N_SEMS,)),
            pltpu.SemaphoreType.DMA((N_SEMS,)),
            pltpu.SemaphoreType.DMA((4,)),
        ],
        name="block_step",
        compiler_params=pltpu.CompilerParams(
            collective_id=0, has_side_effects=True, vmem_limit_bytes=62 << 20
        ),
    )(
        tokens.reshape(ROWS, D),
        cotangent.reshape(ROWS, D),
        in_weight,
        out_weight.T,
        gu_weight,
        down_weight.T,
        conv_weight,
        norm_gains,
    )
    params = (
        (in_weight, in_first, in_second),
        (out_weight.T, out_first.T, out_second.T),
        (gu_weight, gu_first, gu_second),
        (down_weight.T, down_first.T, down_second.T),
        (conv_weight, conv_first, conv_second),
        (norm_gains, gains_first, gains_second),
    )
    grads = (grad_in, grad_out, grad_gu, grad_dn, grad_small)
    big = pl.BlockSpec((CHUNK, D), lambda i: (i, 0))

    def rows_of(array):
        if array.ndim == 3:
            return pl.BlockSpec((array.shape[0], 8, array.shape[2]), lambda i: (0, i, 0))
        if array.shape[0] == 32:
            return pl.BlockSpec((8, array.shape[1]), lambda i: (i, 0))
        return pl.BlockSpec(array.shape, lambda i: (0, 0))

    flat_params = [array for group in params for array in group]
    specs = [rows_of(array) for array in flat_params]
    done = pl.pallas_call(
        finish,
        grid=(4,),
        out_shape=[shape((ROWS, D), f32)] * 2 + [shape(v.shape, f32) for v in flat_params],
        in_specs=[big, big] + [rows_of(v) for v in grads] + specs,
        out_specs=[big, big] + specs,
        name="finish",
    )(mixed.reshape(ROWS, D), tg.reshape(ROWS, D), *grads, *flat_params)
    news = [done[2 + 3 * k : 5 + 3 * k] for k in range(6)]
    return (
        done[0].reshape(tokens.shape),
        done[1].reshape(tokens.shape),
        *news[0],
        *(v.T for v in news[1]),
        *news[2],
        *(v.T for v in news[3]),
        *news[4],
        *news[5],
    )


def solution(mesh):
    rows = P("dp", "seq", None)
    stack = P(None, ("dp", "seq"), "mp")
    flat = P("mp", ("dp", "seq"))
    thin = P(None, ("dp", "seq"))
    groups = (stack,) * 3 + (flat,) * 3 + (stack,) * 3 + (flat,) * 3 + (thin,) * 6
    return jax.shard_map(
        local,
        mesh=mesh,
        in_specs=(rows, rows) + groups,
        out_specs=(rows, rows) + groups,
        check_vma=False,
    )
```

```python
import jax
import jax.numpy as jnp
from jax import lax
from jax.experimental import pallas as pl
from jax.experimental.pallas import tpu as pltpu
from jax.sharding import PartitionSpec as P

STEP = 10

beta_one = 0.9
beta_two = 0.95
eps_adam = 1e-08
eps_norm = 1e-05
rate_matrix = 0.05
rate_small = 0.3
decay_matrix = 0.1

MESH = pl.DeviceIdType.MESH
bf16 = jnp.bfloat16
f32 = jnp.float32

ROWS = 512
CHUNK = 128
D = 1024
CH = 256
FF = 1152
IN0, SM0, OUT0, GU0, DN0, COLS = 0, 768, 896, 1152, 3456, 4608
GRAD_OUT0 = 768


def adamw(master, first, second, grad, rate, decay):
    moment = beta_one * first + (1.0 - beta_one) * grad
    square = beta_two * second + (1.0 - beta_two) * grad * grad
    moment_hat = moment / (1.0 - beta_one**STEP)
    square_hat = square / (1.0 - beta_two**STEP)
    renewed = master - rate * (moment_hat / (jnp.sqrt(square_hat) + eps_adam) + decay * master)
    return (renewed, moment, square)


def rms_scale(values):
    return lax.rsqrt(jnp.mean(values * values, axis=-1, keepdims=True) + eps_norm)


def dot_nn(a, b):
    return jnp.dot(a, b, preferred_element_type=f32)


def dot_nt(a, b):
    return lax.dot_general(a, b, (((1,), (1,)), ((), ())), preferred_element_type=f32)


def dot_tn(a, b):
    return lax.dot_general(a, b, (((0,), (0,)), ((), ())), preferred_element_type=f32)


N_SEMS = 176


def kernel(
    tok_h,
    cot_h,
    w_in,
    w_out,
    w_gu,
    w_dn,
    w_conv,
    w_gain,
    mixed_o,
    tg_o,
    g_in,
    g_out,
    g_gu,
    g_dn,
    small_o,
    tok,
    cot,
    htok,
    square,
    W,
    G,
    RC,
    RX,
    T,
    RZ,
    act1,
    ulow,
    act2,
    rlow,
    hid,
    GG,
    b_s,
    c_s,
    x_s,
    conv_s,
    xext,
    gext,
    mxb,
    gated,
    GB,
    hb,
    smw,
    SM,
    SMR,
    PY,
    RY,
    OWN,
    res_s,
    mixrow,
    tgrow,
    ssem,
    rsem,
    lsem,
):
    z = lax.axis_index("dp")
    seq = lax.axis_index("seq")
    y = lax.axis_index("mp")
    x = seq // 2
    c = lax.rem(seq, 2)
    oc = 1 - c

    def near(value, step):
        return lax.rem(value + step, 4)

    def to_x(step):
        return (z, near(x, step) * 2 + c, y)

    def to_z(step):
        return (near(z, step), seq, y)

    def to_y(step):
        return (z, seq, near(y, step))

    to_core = (z, x * 2 + oc, y)
    to_next = (z, lax.rem(seq + 1, 8), y)
    to_prev = (z, lax.rem(seq + 7, 8), y)

    counter = [0]
    pending = []

    def send(src, dst, where):
        i = counter[0]
        assert i < N_SEMS
        counter[0] += 1
        copy = pltpu.make_async_remote_copy(
            src, dst, ssem.at[i], rsem.at[i], device_id=where, device_id_type=MESH
        )
        copy.start()
        pending.append(copy)
        return copy

    def arrived(copies):
        for copy in copies:
            copy.wait_recv()

    barrier = pltpu.get_barrier_semaphore()
    peers = [to_core, to_next, to_prev]
    for step in (1, 2, 3):
        peers += [to_x(step), to_z(step), to_y(step)]
    for peer in peers:
        pl.semaphore_signal(barrier, inc=1, device_id=peer, device_id_type=MESH)
    load_tok = pltpu.make_async_copy(tok_h, tok, lsem.at[2])
    load_tok.start()
    load_cot = pltpu.make_async_copy(cot_h, cot, lsem.at[3])
    load_cot.start()

    for k in range(3):
        W[z, x, c, :, CH * k : CH * k + CH] = w_in[k].astype(bf16)
    W[z, x, c, :, OUT0:GU0] = w_out[...].astype(bf16)
    square[...] = jnp.zeros((128, 128), f32)
    square[0:3, 0:32] = w_conv[...]
    square[3:5, 0:32] = w_gain[...]
    W[z, x, c, :, SM0:OUT0] = square[...].T[0:32].astype(bf16)
    pl.semaphore_wait(barrier, len(peers))

    def ag_one(lo, mid, hi):
        a, b = pl.ds(lo, mid - lo), pl.ds(mid, hi - mid)
        src_a, src_b = W.at[z, x, c, :, a], W.at[z, x, c, :, b]
        return (
            [send(src_a, src_a, to_x(s)) for s in (1, 3, 2)],
            [send(src_b, src_b, to_z(s)) for s in (1, 3, 2)],
        )

    def ag_two(copies, lo, mid, hi):
        a, b = pl.ds(lo, mid - lo), pl.ds(mid, hi - mid)
        src_a, src_b = W.at[z, :, c, :, a], W.at[:, x, c, :, b]
        arrived(copies[0])
        first = [send(src_a, src_a, to_z(s)) for s in (1, 3)]
        arrived(copies[1])
        return first, [send(src_b, src_b, to_x(s)) for s in (1, 3)]

    def ag_pass(copies, lo, mid, hi):
        a, b = pl.ds(lo, mid - lo), pl.ds(mid, hi - mid)
        low, high = pl.ds(0, 2), pl.ds(2, 2)
        out = []
        for s, half in ((1, low), (3, high)):
            i = 0 if s == 1 else 1
            arrived([copies[0][i]])
            src = W.at[near(z, 4 - s), half, c, :, a]
            out += [send(src, src, to_z(s))]
            arrived([copies[1][i]])
            src = W.at[half, near(x, 4 - s), c, :, b]
            out += [send(src, src, to_x(s))]
        return out

    def ag_three(copies, lo, hi):
        arrived(copies)
        src = W.at[:, :, c, :, pl.ds(lo, hi - lo)]
        return [send(src, src, to_core)]

    def ag_two_direct(copies, lo, mid, hi):
        a, b = pl.ds(lo, mid - lo), pl.ds(mid, hi - mid)
        src_a, src_b = W.at[z, :, c, :, a], W.at[:, x, c, :, b]
        arrived(copies[0])
        first = [send(src_a, src_a, to_z(s)) for s in (1, 3, 2)]
        arrived(copies[1])
        second = [send(src_b, src_b, to_x(s)) for s in (1, 3, 2)]
        core = [send(src_a, src_a, to_core), send(src_b, src_b, to_core)]
        return first, second, core

    def ag_three_direct(copies, lo, mid, hi):
        a, b = pl.ds(lo, mid - lo), pl.ds(mid, hi - mid)
        first, second, core = copies
        for k, s in enumerate((1, 3, 2)):
            arrived([first[k]])
            src = W.at[near(z, 4 - s), :, c, :, a]
            core = core + [send(src, src, to_core)]
            arrived([second[k]])
            src = W.at[:, near(x, 4 - s), c, :, b]
            core = core + [send(src, src, to_core)]
        return core

    g0 = (IN0, 512, OUT0)
    go = (OUT0, OUT0 + 128, GU0)
    g1 = (GU0, GU0 + 1152, DN0)
    g2 = (DN0, DN0 + 640, COLS)
    ag0 = ag_one(*g0)
    ago = ag_one(*go)
    halo = send(tok_h.at[pl.ds(ROWS - 16, 16)], htok, to_next)
    for t in range(9):
        for k in range(2):
            at = GU0 + 256 * t + 128 * k
            W[z, x, c, :, at : at + 128] = w_gu[k, :, 128 * t : 128 * t + 128].astype(bf16)
    W[z, x, c, :, DN0:COLS] = w_dn[...].astype(bf16)
    ag0 = ag_two_direct(ag0, *g0)
    ago = ag_two_direct(ago, *go)
    ag1 = ag_one(*g1)
    ag2 = ag_one(*g2)
    load_tok.wait()
    for i in range(4):
        v = tok[CHUNK * i : CHUNK * i + CHUNK]
        OWN[i] = v * rms_scale(v)
    ag0 = ag_three_direct(ag0, *g0)
    ag1 = ag_two(ag1, *g1)
    load_cot.wait()
    for r in range(0, ROWS, 128):
        ulow[r : r + 128] = cot[r : r + 128].astype(bf16)
    ago = ag_three_direct(ago, *go)
    arrived(ag0)

    def weights(lo, n):
        return W[:, :, :, :, pl.ds(lo, n)].reshape(D, n)

    def weight_rows(block, lo, n):
        return W[block, :, :, :, pl.ds(lo, n)].reshape(256, n)

    smw[...] = weights(SM0, 128).astype(f32).T[:8]
    gain_one = smw[3:4]
    gain_two = smw[4:5]
    own_channels = pl.ds(pl.multiple_of(y * CH, CH), CH)
    taps = smw[:, own_channels]
    tap0, tap1, tap2 = taps[0:1], taps[1:2], taps[2:3]

    for i in range(4):
        act1[CHUNK * i + 16 : CHUNK * i + 144] = (OWN[i] * gain_one).astype(bf16)
    arrived([halo])
    v = htok[...]
    act1[0:16] = (v * rms_scale(v) * gain_one).astype(bf16)
    bgate = dot_nn(act1[...], weights(0, CH))
    xvalue = dot_nn(act1[...], weights(2 * CH, CH))
    xext[...] = (bgate * xvalue).astype(bf16).astype(f32)
    b_s[...] = bgate[16:]
    x_s[...] = xvalue[16:]
    xext[0:16] = jnp.where(seq > 0, xext[0:16], 0.0)
    c_s[...] = dot_nn(act1[16:], weights(CH, CH))
    conv_s[...] = (
        tap0 * xext[14 : ROWS + 14] + tap1 * xext[15 : ROWS + 15] + tap2 * xext[16 : ROWS + 16]
    )
    gated[...] = (c_s[...] * conv_s[...]).astype(bf16)
    arrived(ago)

    def chunk_rows(step):
        return pl.ds(pl.multiple_of(near(y, step) * CHUNK, CHUNK), CHUNK)

    def partial(which, steps, values, lo, n):
        for block in range(4):
            part = dot_nt(values, weight_rows(block, lo, n))
            cols = slice(block * 256, block * 256 + 256)
            for k, step in enumerate(steps):
                piece = part[CHUNK * k : CHUNK * k + CHUNK]
                if step == 0:
                    OWN[which, :, cols] = piece
                else:
                    PY[which, step - 1, :, cols] = piece.astype(bf16)
        return [
            send(PY.at[which, step - 1], RY.at[which, step - 1], to_y(step))
            for step in steps
            if step
        ]

    half = CHUNK // 2
    low_half, high_half = pl.ds(0, half), pl.ds(half, half)

    def part_of(which, slot, rows, where):
        return send(PY.at[which, slot, rows], RY.at[which, slot, rows], where)

    def rs_y(which, source, lo, n):
        def block_of(step):
            return source[chunk_rows(step)]

        for step in (2, 1, 3, 0):
            values = block_of(step)
            for block in range(4):
                part = dot_nt(values, weight_rows(block, lo, n))
                cols = slice(block * 256, block * 256 + 256)
                if step == 0:
                    OWN[which, :, cols] = part
                else:
                    PY[which, step - 1, :, cols] = part.astype(bf16)
            if step == 2:
                relay = (
                    part_of(which, 1, low_half, to_y(1)),
                    part_of(which, 1, high_half, to_y(3)),
                )
            elif step == 1:
                direct = [part_of(which, 0, high_half, to_y(1))]
            elif step == 3:
                direct += [part_of(which, 2, low_half, to_y(3))]
        return relay, direct

    def rs_y_pass(which, state):
        relay, direct = state
        out = list(direct)
        for k, (slot, rows, where) in enumerate(
            ((0, slice(0, half), to_y(1)), (2, slice(half, CHUNK), to_y(3)))
        ):
            arrived([relay[k]])
            PY[which, slot, rows] = (
                PY[which, slot, rows].astype(f32) + RY[which, 1, rows].astype(f32)
            ).astype(bf16)
            out += [part_of(which, slot, low_half if k == 0 else high_half, where)]
        return out

    def summed_relayed(which, copies):
        arrived(copies)
        return OWN[which] + RY[which, 0].astype(f32) + RY[which, 2].astype(f32)

    def summed(which, copies):
        arrived(copies)
        return (
            OWN[which]
            + RY[which, 0].astype(f32)
            + RY[which, 1].astype(f32)
            + RY[which, 2].astype(f32)
        )

    def ag_y(src, slot):
        return (send(src, slot(y), to_y(1)), send(src, slot(y), to_y(3)))

    def ag_y_pass(copies, slot):
        arrived(copies[:1])
        left = slot(near(y, 3)).at[pl.ds(0, half)]
        out = [send(left, left, to_y(1))]
        arrived(copies[1:])
        right = slot(near(y, 1)).at[pl.ds(half, half)]
        return out + [send(right, right, to_y(3))]

    rs = rs_y(0, gated, OUT0, CH)
    ag2 = ag_two(ag2, *g2)
    ag1 = ag_pass(ag1, *g1)
    rs = rs_y_pass(0, rs)
    ag2 = ag_pass(ag2, *g2)
    ag1 = ag_three(ag1, GU0, DN0)
    ag2 = ag_three(ag2, DN0, COLS)

    own_rows = chunk_rows(0)
    resid = tok[own_rows] + summed_relayed(0, rs)
    res_s[...] = resid
    act2[y] = (resid * rms_scale(resid) * gain_two).astype(bf16)
    def act2_slot(i):
        return act2.at[i]

    ag_act2 = ag_y(act2.at[y], act2_slot)
    arrived(ag1)
    arrived(ag2)

    def ffn_part(acts, ups, rows, f_lo, n):
        gu = dot_nn(acts, weights(GU0 + 2 * f_lo, 2 * n))
        gh = dot_nn(ups, weights(DN0 + f_lo, n))
        for j in range(n // 128):
            gate = gu[:, 256 * j : 256 * j + 128]
            up = gu[:, 256 * j + 128 : 256 * j + 256]
            grad = gh[:, 128 * j : 128 * j + 128]
            sig = jax.nn.sigmoid(gate)
            swish = gate * sig
            hidden = (swish * up).astype(bf16)
            grad_gate = (grad * up * sig * (1.0 + gate * (1.0 - sig))).astype(bf16)
            grad_up = (grad * swish).astype(bf16)
            for k, here in enumerate(rows):
                piece = slice(CHUNK * k, CHUNK * k + CHUNK)
                hid[here, pl.ds(f_lo + 128 * j, 128)] = hidden[piece]
                GG[here, pl.ds(2 * f_lo + 256 * j, 128)] = grad_gate[piece]
                GG[here, pl.ds(2 * f_lo + 256 * j + 128, 128)] = grad_up[piece]

    def stacked(parts):
        return parts[0] if len(parts) == 1 else jnp.concatenate(parts, axis=0)

    rs = []
    for steps in ((0,), (1, 3), (2,)):
        if steps == (1, 3):
            ag_act2 = ag_y_pass(ag_act2, act2_slot)
        if steps == (2,):
            arrived(ag_act2)
        rows = [chunk_rows(step) for step in steps]
        acts = stacked([act2[near(y, step)] for step in steps])
        ups = stacked([ulow[here] for here in rows])

        @pl.loop(0, 4)
        def _(t):
            ffn_part(acts, ups, rows, pl.multiple_of(t * 256, 256), 256)

        ffn_part(acts, ups, rows, 1024, 128)
        rs += partial(1, steps, stacked([GG[here] for here in rows]), GU0, 2 * FF)

    def weight_grad(left, right, lo, n):
        for block in range(4):
            values = left(block)
            for start in range(0, n, 384):
                width = min(384, n - start)
                part = dot_tn(values, right[:, pl.ds(start, width)])
                G[block, :, :, :, pl.ds(lo + start, width)] = part.astype(bf16).reshape(
                    4, 2, 32, width
                )

    def rs_core(lo, hi):
        cols = pl.ds(lo, hi - lo)
        return [send(G.at[:, :, oc, :, cols], RC.at[:, :, :, cols], to_core)]

    def rs_one(copies, lo, mid, hi):
        arrived(copies)
        cols = pl.ds(lo, hi - lo)

        @pl.loop(0, 4)
        def _(i):
            for j in range(4):
                G[i, j, c, :, cols] = (
                    G[i, j, c, :, cols].astype(f32) + RC[i, j, :, cols].astype(f32)
                ).astype(bf16)

        a, b = pl.ds(lo, mid - lo), pl.ds(mid, hi - mid)
        out = []
        for s in (1, 3, 2):
            out += [send(G.at[:, near(x, s), c, :, a], RX.at[s - 1, :, :, a], to_x(s))]
            out += [send(G.at[near(z, s), :, c, :, b], RX.at[s - 1, :, :, b], to_z(s))]
        return out

    def rs_two(copies, lo, mid, hi):
        arrived(copies)
        a, b = pl.ds(lo, mid - lo), pl.ds(mid, hi - mid)

        @pl.loop(0, 4)
        def _(i):
            T[i, :, a] = (
                G[i, x, c, :, a].astype(f32)
                + RX[0, i, :, a].astype(f32)
                + RX[1, i, :, a].astype(f32)
                + RX[2, i, :, a].astype(f32)
            ).astype(bf16)
            T[i, :, b] = (
                G[z, i, c, :, b].astype(f32)
                + RX[0, i, :, b].astype(f32)
                + RX[1, i, :, b].astype(f32)
                + RX[2, i, :, b].astype(f32)
            ).astype(bf16)

        out = []
        for s in (1, 3, 2):
            out += [send(T.at[near(z, s), :, a], RZ.at[s - 1, :, a], to_z(s))]
            out += [send(T.at[near(x, s), :, b], RZ.at[s - 1, :, b], to_x(s))]
        return out

    def rs_end(lo, n, mid):
        cols = pl.ds(lo, n)
        mine = z if lo < mid else x
        return (
            T[mine, :, cols].astype(f32)
            + RZ[0, :, cols].astype(f32)
            + RZ[1, :, cols].astype(f32)
            + RZ[2, :, cols].astype(f32)
        )

    gi = (IN0, 512, 1024)
    rs_ffn = rs_y(2, hid, DN0, FF)

    back_two = summed(1, rs)
    resid = res_s[...]
    scale_two = rms_scale(resid)
    normed = resid * scale_two
    SM[0] = jnp.zeros((8, D), f32)
    SM[0, 4:5] = jnp.sum(back_two * normed, axis=0, keepdims=True)
    scaled = back_two * gain_two
    grad_resid = cot[own_rows] + scale_two * (
        scaled - normed * jnp.mean(scaled * normed, axis=-1, keepdims=True)
    )
    rlow[y] = grad_resid.astype(bf16)

    def rlow_slot(i):
        return rlow.at[i]

    ag_rlow = ag_y(rlow.at[y], rlow_slot)
    OWN[1] = grad_resid

    weight_grad(
        lambda i: act2[:, :, i * 256 : i * 256 + 256].reshape(ROWS, 256), GG, GU0, 2 * FF
    )
    r_gu = rs_core(GU0, DN0)
    ag_rlow = ag_y_pass(ag_rlow, rlow_slot)
    rs_ffn = rs_y_pass(2, rs_ffn)
    weight_grad(lambda i: ulow[:, i * 256 : i * 256 + 256], hid, DN0, FF)
    r_dn = rs_core(DN0, COLS)
    r_gu = rs_one(r_gu, *g1)

    arrived(ag_rlow)

    mixrow[...] = (res_s[...] + summed_relayed(2, rs_ffn)).astype(bf16)

    def mixed_slot(i):
        return mixed_o.at[i]

    ag_mixed = ag_y(mixrow, mixed_slot)
    local_mixed = pltpu.make_async_copy(mixrow, mixed_o.at[y], lsem.at[0])
    local_mixed.start()
    low = rlow[...].reshape(ROWS, D)
    grad_gated = dot_nn(low, weights(OUT0, CH))
    gext[0:ROWS] = (grad_gated * c_s[...]).astype(bf16).astype(f32)
    mxb[...] = gext[0:16].astype(bf16)
    halo = send(mxb, hb, to_prev)
    GB[:, CH : 2 * CH] = (grad_gated * conv_s[...]).astype(bf16)
    grad_conv = gext[0:ROWS]
    for k in range(3):
        row = jnp.sum(grad_conv * xext[14 + k : ROWS + 14 + k], axis=0, keepdims=True)
        SM[0, k : k + 1, own_channels] = row
    weight_grad(
        lambda i: rlow[:, :, i * 256 : i * 256 + 256].reshape(ROWS, 256), gated, GRAD_OUT0, CH
    )
    arrived([halo])
    gext[ROWS : ROWS + 8] = jnp.where(seq < 7, hb[...].astype(f32)[0:8], 0.0)
    grad_mixed = tap2 * gext[0:ROWS] + tap1 * gext[1 : ROWS + 1] + tap0 * gext[2 : ROWS + 2]
    GB[:, 0:CH] = (grad_mixed * x_s[...]).astype(bf16)
    GB[:, 2 * CH : 3 * CH] = (grad_mixed * b_s[...]).astype(bf16)

    rs = rs_y(3, GB, IN0, 3 * CH)
    weight_grad(lambda i: act1[16:, i * 256 : i * 256 + 256], GB, IN0, 3 * CH)
    r_in = rs_core(IN0, 1024)
    r_dn = rs_one(r_dn, *g2)
    rs = rs_y_pass(3, rs)
    ag_mixed = ag_y_pass(ag_mixed, mixed_slot)

    r_in = rs_one(r_in, *gi)

    back_one = summed_relayed(3, rs)
    own_tok = tok[own_rows]
    scale_one = rms_scale(own_tok)
    normed = own_tok * scale_one
    SM[0, 3:4] = jnp.sum(back_one * normed, axis=0, keepdims=True)
    scaled = back_one * gain_one
    tgrow[...] = (
        OWN[1]
        + scale_one * (scaled - normed * jnp.mean(scaled * normed, axis=-1, keepdims=True))
    ).astype(bf16)

    def tg_slot(i):
        return tg_o.at[i]

    ag_tg = ag_y(tgrow, tg_slot)
    local_tg = pltpu.make_async_copy(tgrow, tg_o.at[y], lsem.at[1])
    local_tg.start()

    sm = [send(SM.at[0], SMR.at[0], to_core)]
    r_gu = rs_two(r_gu, *g1)
    r_dn = rs_two(r_dn, *g2)
    arrived(sm)
    SM[1] = SM[0] + SMR[0]
    sm = [send(SM.at[1], SMR.at[s], to_x(s)) for s in (1, 3, 2)]

    arrived(r_dn)
    g_dn[:, 0:640] = rs_end(DN0, 640, g2[1])
    g_dn[:, 640:1152] = rs_end(DN0 + 640, 512, g2[1])

    r_in = rs_two(r_in, *gi)
    arrived(sm)
    SM[2] = SM[1] + SMR[1] + SMR[2] + SMR[3]
    sm = [send(SM.at[2], SMR.at[3 + s], to_z(s)) for s in (1, 3, 2)]

    ag_tg = ag_y_pass(ag_tg, tg_slot)
    arrived(r_gu)
    for t in range(9):
        g_gu[0, :, 128 * t : 128 * t + 128] = rs_end(GU0 + 256 * t, 128, g1[1])
        g_gu[1, :, 128 * t : 128 * t + 128] = rs_end(GU0 + 256 * t + 128, 128, g1[1])

    arrived(sm)
    SMR[7] = SM[2] + SMR[4] + SMR[5] + SMR[6]
    sm = [send(SMR.at[7], SMR.at[7 + s], to_y(s)) for s in (1, 3, 2)]

    arrived(r_in)
    for k in range(3):
        g_in[k] = rs_end(IN0 + CH * k, CH, gi[1])
    g_out[...] = rs_end(GRAD_OUT0, CH, gi[1])

    arrived(sm)

    def term(j):
        return SMR[7 + lax.rem(y - j + 4, 4)]

    shard_at = z * 8 + seq
    SMR[0] = ((term(0) + term(1)) + term(2)) + term(3)
    four = SMR[0, :, pl.ds(pl.multiple_of(shard_at // 4 * 128, 128), 128)]
    place = lax.rem(shard_at, 4)
    mine = four[:, 0:32]
    for k in range(1, 4):
        mine = jnp.where(place == k, four[:, 32 * k : 32 * k + 32], mine)
    small_o[...] = mine

    arrived(ag_mixed)
    arrived(ag_tg)
    local_mixed.wait()
    local_tg.wait()
    for copy in pending:
        copy.wait_send()


def finish(*refs):
    refs[25][...] = refs[0][...].astype(f32)
    refs[26][...] = refs[1][...].astype(f32)
    small = refs[6][...]
    grads = [ref[...] for ref in refs[2:6]] + [small[0:3], small[3:5]]
    for k, grad in enumerate(grads):
        rate, decay = (rate_matrix, decay_matrix) if k < 4 else (rate_small, 0.0)
        group = refs[7 + 3 * k : 10 + 3 * k]
        new = adamw(*(ref[...] for ref in group), grad, rate, decay)
        for ref, value in zip(refs[27 + 3 * k : 30 + 3 * k], new):
            ref[...] = value


def local(
    tokens,
    cotangent,
    in_weight,
    in_first,
    in_second,
    out_weight,
    out_first,
    out_second,
    gu_weight,
    gu_first,
    gu_second,
    down_weight,
    down_first,
    down_second,
    conv_weight,
    conv_first,
    conv_second,
    norm_gains,
    gains_first,
    gains_second,
):
    vmem = pl.BlockSpec(memory_space=pltpu.VMEM)
    hbm = pl.BlockSpec(memory_space=pl.ANY)
    shape = jax.ShapeDtypeStruct
    mixed, tg, grad_in, grad_out, grad_gu, grad_dn, grad_small = pl.pallas_call(
        kernel,
        out_shape=(
            shape((4, CHUNK, D), bf16),
            shape((4, CHUNK, D), bf16),
            shape((3, 32, CH), f32),
            shape((32, CH), f32),
            shape((2, 32, FF), f32),
            shape((32, FF), f32),
            shape((8, 32), f32),
        ),
        in_specs=[hbm] * 2 + [vmem] * 6,
        out_specs=(hbm, hbm, vmem, vmem, vmem, vmem, vmem),
        scratch_shapes=[
            pltpu.VMEM((ROWS, D), f32),
            pltpu.VMEM((ROWS, D), f32),
            pltpu.VMEM((16, D), f32),
            pltpu.VMEM((128, 128), f32),
            pltpu.VMEM((4, 4, 2, 32, COLS), bf16),
            pltpu.VMEM((4, 4, 2, 32, COLS), bf16),
            pltpu.VMEM((4, 4, 32, COLS), bf16),
            pltpu.VMEM((3, 4, 32, COLS), bf16),
            pltpu.VMEM((4, 32, COLS), bf16),
            pltpu.VMEM((3, 32, COLS), bf16),
            pltpu.VMEM((ROWS + 16, D), bf16),
            pltpu.VMEM((ROWS, D), bf16),
            pltpu.VMEM((4, CHUNK, D), bf16),
            pltpu.VMEM((4, CHUNK, D), bf16),
            pltpu.VMEM((ROWS, FF), bf16),
            pltpu.VMEM((ROWS, 2 * FF), bf16),
            pltpu.VMEM((ROWS, CH), f32),
            pltpu.VMEM((ROWS, CH), f32),
            pltpu.VMEM((ROWS, CH), f32),
            pltpu.VMEM((ROWS, CH), f32),
            pltpu.VMEM((ROWS + 16, CH), f32),
            pltpu.VMEM((ROWS + 8, CH), f32),
            pltpu.VMEM((16, CH), bf16),
            pltpu.VMEM((ROWS, CH), bf16),
            pltpu.VMEM((ROWS, 3 * CH), bf16),
            pltpu.VMEM((16, CH), bf16),
            pltpu.VMEM((8, D), f32),
            pltpu.VMEM((3, 8, D), f32),
            pltpu.VMEM((11, 8, D), f32),
            pltpu.VMEM((4, 3, CHUNK, D), bf16),
            pltpu.VMEM((4, 3, CHUNK, D), bf16),
            pltpu.VMEM((4, CHUNK, D), f32),
            pltpu.VMEM((CHUNK, D), f32),
            pltpu.VMEM((CHUNK, D), bf16),
            pltpu.VMEM((CHUNK, D), bf16),
            pltpu.SemaphoreType.DMA((N_SEMS,)),
            pltpu.SemaphoreType.DMA((N_SEMS,)),
            pltpu.SemaphoreType.DMA((4,)),
        ],
        name="block_step",
        compiler_params=pltpu.CompilerParams(
            collective_id=0, has_side_effects=True, vmem_limit_bytes=62 << 20
        ),
    )(
        tokens.reshape(ROWS, D),
        cotangent.reshape(ROWS, D),
        in_weight,
        out_weight.T,
        gu_weight,
        down_weight.T,
        conv_weight,
        norm_gains,
    )
    params = (
        (in_weight, in_first, in_second),
        (out_weight.T, out_first.T, out_second.T),
        (gu_weight, gu_first, gu_second),
        (down_weight.T, down_first.T, down_second.T),
        (conv_weight, conv_first, conv_second),
        (norm_gains, gains_first, gains_second),
    )
    grads = (grad_in, grad_out, grad_gu, grad_dn, grad_small)
    big = pl.BlockSpec((CHUNK, D), lambda i: (i, 0))

    def rows_of(array):
        if array.ndim == 3:
            return pl.BlockSpec((array.shape[0], 8, array.shape[2]), lambda i: (0, i, 0))
        if array.shape[0] == 32:
            return pl.BlockSpec((8, array.shape[1]), lambda i: (i, 0))
        return pl.BlockSpec(array.shape, lambda i: (0, 0))

    flat_params = [array for group in params for array in group]
    specs = [rows_of(array) for array in flat_params]
    done = pl.pallas_call(
        finish,
        grid=(4,),
        out_shape=[shape((ROWS, D), f32)] * 2 + [shape(v.shape, f32) for v in flat_params],
        in_specs=[big, big] + [rows_of(v) for v in grads] + specs,
        out_specs=[big, big] + specs,
        name="finish",
    )(mixed.reshape(ROWS, D), tg.reshape(ROWS, D), *grads, *flat_params)
    news = [done[2 + 3 * k : 5 + 3 * k] for k in range(6)]
    return (
        done[0].reshape(tokens.shape),
        done[1].reshape(tokens.shape),
        *news[0],
        *(v.T for v in news[1]),
        *news[2],
        *(v.T for v in news[3]),
        *news[4],
        *news[5],
    )


def solution(mesh):
    rows = P("dp", "seq", None)
    stack = P(None, ("dp", "seq"), "mp")
    flat = P("mp", ("dp", "seq"))
    thin = P(None, ("dp", "seq"))
    groups = (stack,) * 3 + (flat,) * 3 + (stack,) * 3 + (flat,) * 3 + (thin,) * 6
    return jax.shard_map(
        local,
        mesh=mesh,
        in_specs=(rows, rows) + groups,
        out_specs=(rows, rows) + groups,
        check_vma=False,
    )
```

```python
import jax
import jax.numpy as jnp
from jax import lax
from jax.experimental import pallas as pl
from jax.experimental.pallas import tpu as pltpu
from jax.sharding import PartitionSpec as P

STEP = 10

beta_one = 0.9
beta_two = 0.95
eps_adam = 1e-08
eps_norm = 1e-05
rate_matrix = 0.05
rate_small = 0.3
decay_matrix = 0.1

MESH = pl.DeviceIdType.MESH
bf16 = jnp.bfloat16
f32 = jnp.float32

ROWS = 512
CHUNK = 128
D = 1024
CH = 256
FF = 1152
IN0, SM0, OUT0, GU0, DN0, COLS = 0, 768, 896, 1152, 3456, 4608
GRAD_OUT0 = 768


def adamw(master, first, second, grad, rate, decay):
    moment = beta_one * first + (1.0 - beta_one) * grad
    square = beta_two * second + (1.0 - beta_two) * grad * grad
    moment_hat = moment / (1.0 - beta_one**STEP)
    square_hat = square / (1.0 - beta_two**STEP)
    renewed = master - rate * (moment_hat / (jnp.sqrt(square_hat) + eps_adam) + decay * master)
    return (renewed, moment, square)


def rms_scale(values):
    return lax.rsqrt(jnp.mean(values * values, axis=-1, keepdims=True) + eps_norm)


def dot_nn(a, b):
    return jnp.dot(a, b, preferred_element_type=f32)


def dot_nt(a, b):
    return lax.dot_general(a, b, (((1,), (1,)), ((), ())), preferred_element_type=f32)


def dot_tn(a, b):
    return lax.dot_general(a, b, (((0,), (0,)), ((), ())), preferred_element_type=f32)


N_SEMS = 192


def kernel(
    tok_h,
    cot_h,
    w_in,
    w_out,
    w_gu,
    w_dn,
    w_conv,
    w_gain,
    mixed_o,
    tg_o,
    g_in,
    g_out,
    g_gu,
    g_dn,
    small_o,
    tok,
    cot,
    htok,
    square,
    W,
    G,
    RC,
    RX,
    T,
    RZ,
    act1,
    ulow,
    act2,
    rlow,
    hid,
    GG,
    b_s,
    c_s,
    x_s,
    conv_s,
    xext,
    gext,
    hlow,
    gated,
    GB,
    c_after,
    smw,
    SM,
    SMR,
    PY,
    RY,
    OWN,
    res_s,
    own_tok,
    mixrow,
    tgrow,
    ssem,
    rsem,
    lsem,
):
    z = lax.axis_index("dp")
    seq = lax.axis_index("seq")
    y = lax.axis_index("mp")
    x = seq // 2
    c = lax.rem(seq, 2)
    oc = 1 - c

    def near(value, step):
        return lax.rem(value + step, 4)

    def to_x(step):
        return (z, near(x, step) * 2 + c, y)

    def to_z(step):
        return (near(z, step), seq, y)

    def to_y(step):
        return (z, seq, near(y, step))

    to_core = (z, x * 2 + oc, y)
    to_next = (z, lax.rem(seq + 1, 8), y)
    to_prev = (z, lax.rem(seq + 7, 8), y)

    counter = [0]
    pending = []

    def send(src, dst, where):
        i = counter[0]
        assert i < N_SEMS
        counter[0] += 1
        copy = pltpu.make_async_remote_copy(
            src, dst, ssem.at[i], rsem.at[i], device_id=where, device_id_type=MESH
        )
        copy.start()
        pending.append(copy)
        return copy

    def arrived(copies):
        for copy in copies:
            copy.wait_recv()

    barrier = pltpu.get_barrier_semaphore()
    peers = [to_core, to_prev] + [(z, lax.rem(seq + 1, 8), k) for k in range(4)]
    for step in (1, 2, 3):
        peers += [to_x(step), to_z(step), to_y(step)]
    for peer in peers:
        pl.semaphore_signal(barrier, inc=1, device_id=peer, device_id_type=MESH)
    load_tok = pltpu.make_async_copy(tok_h, tok, lsem.at[2])
    load_tok.start()
    load_cot = pltpu.make_async_copy(cot_h, cot, lsem.at[3])
    load_cot.start()

    for k in range(3):
        W[z, x, c, :, CH * k : CH * k + CH] = w_in[k].astype(bf16)
    W[z, x, c, :, OUT0:GU0] = w_out[...].astype(bf16)
    square[...] = jnp.zeros((128, 128), f32)
    square[0:3, 0:32] = w_conv[...]
    square[3:5, 0:32] = w_gain[...]
    W[z, x, c, :, SM0:OUT0] = square[...].T[0:32].astype(bf16)
    pl.semaphore_wait(barrier, len(peers))

    def ag_one(lo, mid, hi):
        a, b = pl.ds(lo, mid - lo), pl.ds(mid, hi - mid)
        src_a, src_b = W.at[z, x, c, :, a], W.at[z, x, c, :, b]
        return (
            [send(src_a, src_a, to_x(s)) for s in (1, 3, 2)],
            [send(src_b, src_b, to_z(s)) for s in (1, 3, 2)],
        )

    def ag_two(copies, lo, mid, hi):
        a, b = pl.ds(lo, mid - lo), pl.ds(mid, hi - mid)
        src_a, src_b = W.at[z, :, c, :, a], W.at[:, x, c, :, b]
        arrived(copies[0])
        first = [send(src_a, src_a, to_z(s)) for s in (1, 3)]
        arrived(copies[1])
        second = [send(src_b, src_b, to_x(s)) for s in (1, 3)]
        return first, second, [send(src_a, src_a, to_core), send(src_b, src_b, to_core)]

    def ag_pass(copies, lo, mid, hi):
        core = copies[2]
        a, b = pl.ds(lo, mid - lo), pl.ds(mid, hi - mid)
        low, high = pl.ds(0, 2), pl.ds(2, 2)
        out = []
        for s, half in ((1, low), (3, high)):
            i = 0 if s == 1 else 1
            arrived([copies[0][i]])
            src = W.at[near(z, 4 - s), half, c, :, a]
            out += [send(src, src, to_z(s))]
            arrived([copies[1][i]])
            src = W.at[half, near(x, 4 - s), c, :, b]
            out += [send(src, src, to_x(s))]
            src = W.at[near(z, 4 - s), :, c, :, a]
            core = core + [send(src, src, to_core)]
            src = W.at[:, near(x, 4 - s), c, :, b]
            core = core + [send(src, src, to_core)]
        return out, core

    def ag_three(copies, lo, mid, hi):
        a, b = pl.ds(lo, mid - lo), pl.ds(mid, hi - mid)
        arrived(copies[0])
        src_a, src_b = W.at[near(z, 2), :, c, :, a], W.at[:, near(x, 2), c, :, b]
        return copies[1] + [send(src_a, src_a, to_core), send(src_b, src_b, to_core)]

    def ag_two_direct(copies, lo, mid, hi):
        a, b = pl.ds(lo, mid - lo), pl.ds(mid, hi - mid)
        src_a, src_b = W.at[z, :, c, :, a], W.at[:, x, c, :, b]
        arrived(copies[0])
        first = [send(src_a, src_a, to_z(s)) for s in (1, 3, 2)]
        arrived(copies[1])
        second = [send(src_b, src_b, to_x(s)) for s in (1, 3, 2)]
        core = [send(src_a, src_a, to_core), send(src_b, src_b, to_core)]
        return first, second, core

    def ag_three_direct(copies, lo, mid, hi):
        a, b = pl.ds(lo, mid - lo), pl.ds(mid, hi - mid)
        first, second, core = copies
        for k, s in enumerate((1, 3, 2)):
            arrived([first[k]])
            src = W.at[near(z, 4 - s), :, c, :, a]
            core = core + [send(src, src, to_core)]
            arrived([second[k]])
            src = W.at[:, near(x, 4 - s), c, :, b]
            core = core + [send(src, src, to_core)]
        return core

    g0 = (IN0, 512, OUT0)
    go = (OUT0, OUT0 + 128, GU0)
    g1 = (GU0, GU0 + 1152, DN0)
    g2 = (DN0, DN0 + 640, COLS)
    ag0 = ag_one(*g0)
    ago = ag_one(*go)
    halo = [
        send(tok_h.at[pl.ds(ROWS - 16, 16)], htok.at[0], to_next),
        send(tok_h.at[pl.ds(0, 16)], htok.at[1], to_prev),
    ]
    for t in range(9):
        for k in range(2):
            at = GU0 + 256 * t + 128 * k
            W[z, x, c, :, at : at + 128] = w_gu[k, :, 128 * t : 128 * t + 128].astype(bf16)
    W[z, x, c, :, DN0:COLS] = w_dn[...].astype(bf16)
    ag0 = ag_two_direct(ag0, *g0)
    ago = ag_two_direct(ago, *go)
    ag1 = ag_one(*g1)
    ag2 = ag_one(*g2)
    load_tok.wait()
    mine = pl.ds(pl.multiple_of(y * CHUNK, CHUNK), CHUNK)
    own_tok[...] = tok[mine]
    for i in range(4):
        here = slice(CHUNK * i, CHUNK * i + CHUNK)
        v = tok[here]
        tok[here] = v * rms_scale(v)
    ag0 = ag_three_direct(ag0, *g0)
    ag1 = ag_two(ag1, *g1)
    ag2 = ag_two(ag2, *g2)
    load_cot.wait()
    for r in range(0, ROWS, 128):
        ulow[r : r + 128] = cot[r : r + 128].astype(bf16)
    ago = ag_three_direct(ago, *go)
    arrived(ag0)

    def weights(lo, n):
        return W[:, :, :, :, pl.ds(lo, n)].reshape(D, n)

    def weight_rows(block, lo, n):
        return W[block, :, :, :, pl.ds(lo, n)].reshape(256, n)

    smw[...] = weights(SM0, 128).astype(f32).T[:8]
    gain_one = smw[3:4]
    gain_two = smw[4:5]
    own_channels = pl.ds(pl.multiple_of(y * CH, CH), CH)
    taps = smw[:, own_channels]
    tap0, tap1, tap2 = taps[0:1], taps[1:2], taps[2:3]

    for i in range(4):
        act1[CHUNK * i + 16 : CHUNK * i + 144] = (tok[CHUNK * i : CHUNK * i + CHUNK] * gain_one).astype(bf16)
    arrived(halo)
    for i in range(2):
        v = htok[i]
        at = i * (ROWS + 16)
        act1[at : at + 16] = (v * rms_scale(v) * gain_one).astype(bf16)
    bgate = dot_nn(act1[0 : ROWS + 16], weights(0, CH))
    xvalue = dot_nn(act1[0 : ROWS + 16], weights(2 * CH, CH))
    xext[...] = (bgate * xvalue).astype(bf16).astype(f32)
    b_s[...] = bgate[16:]
    x_s[...] = xvalue[16:]
    xext[0:16] = jnp.where(seq > 0, xext[0:16], 0.0)
    cgate = dot_nn(act1[16:], weights(CH, CH))
    c_s[...] = cgate[0:ROWS]
    c_after[...] = cgate[ROWS:]
    conv_s[...] = (
        tap0 * xext[14 : ROWS + 14] + tap1 * xext[15 : ROWS + 15] + tap2 * xext[16 : ROWS + 16]
    )
    gated[...] = (c_s[...] * conv_s[...]).astype(bf16)
    arrived(ago)

    def chunk_rows(step):
        return pl.ds(pl.multiple_of(near(y, step) * CHUNK, CHUNK), CHUNK)

    def partial(which, steps, values, lo, n):
        for block in range(4):
            part = dot_nt(values, weight_rows(block, lo, n))
            cols = slice(block * 256, block * 256 + 256)
            for k, step in enumerate(steps):
                piece = part[CHUNK * k : CHUNK * k + CHUNK]
                if step == 0:
                    OWN[which, :, cols] = piece
                else:
                    PY[which, step - 1, :, cols] = piece.astype(bf16)
        return [
            send(PY.at[which, step - 1], RY.at[which, step - 1], to_y(step))
            for step in steps
            if step
        ]

    half = CHUNK // 2
    low_half, high_half = pl.ds(0, half), pl.ds(half, half)

    def part_of(which, slot, rows, where):
        return send(PY.at[which, slot, rows], RY.at[which, slot, rows], where)

    def rs_y(which, source, lo, n, against=None):
        def block_of(step):
            return source[chunk_rows(step)]

        for step in (2, 1, 3, 0):
            values = block_of(step)
            for block in range(4):
                part = dot_nt(values, weight_rows(block, lo, n))
                cols = slice(block * 256, block * 256 + 256)
                if against is not None:
                    SM[0, 3:4, cols] += jnp.sum(
                        part * against[chunk_rows(step), cols], axis=0, keepdims=True
                    )
                if step == 0:
                    OWN[which, :, cols] = part
                else:
                    PY[which, step - 1, :, cols] = part.astype(bf16)
            if step == 2:
                relay = (
                    part_of(which, 1, low_half, to_y(1)),
                    part_of(which, 1, high_half, to_y(3)),
                )
            elif step == 1:
                direct = [part_of(which, 0, high_half, to_y(1))]
            elif step == 3:
                direct += [part_of(which, 2, low_half, to_y(3))]
        return relay, direct

    def rs_y_pass(which, state):
        relay, direct = state
        out = list(direct)
        for k, (slot, rows, where) in enumerate(
            ((0, slice(0, half), to_y(1)), (2, slice(half, CHUNK), to_y(3)))
        ):
            arrived([relay[k]])
            PY[which, slot, rows] = (
                PY[which, slot, rows].astype(f32) + RY[which, 1, rows].astype(f32)
            ).astype(bf16)
            out += [part_of(which, slot, low_half if k == 0 else high_half, where)]
        return out

    def summed_relayed(which, copies):
        arrived(copies)
        return OWN[which] + RY[which, 0].astype(f32) + RY[which, 2].astype(f32)

    def summed(which, copies):
        arrived(copies)
        return (
            OWN[which]
            + RY[which, 0].astype(f32)
            + RY[which, 1].astype(f32)
            + RY[which, 2].astype(f32)
        )

    def ag_y(src, slot):
        return (send(src, slot(y), to_y(1)), send(src, slot(y), to_y(3)))

    def ag_y_pass(copies, slot):
        arrived(copies[:1])
        left = slot(near(y, 3)).at[pl.ds(0, half)]
        out = [send(left, left, to_y(1))]
        arrived(copies[1:])
        right = slot(near(y, 1)).at[pl.ds(half, half)]
        return out + [send(right, right, to_y(3))]

    rs = rs_y(0, gated, OUT0, CH)
    ag1 = ag_pass(ag1, *g1)
    ag2 = ag_pass(ag2, *g2)
    rs = rs_y_pass(0, rs)
    ag1 = ag_three(ag1, *g1)
    ag2 = ag_three(ag2, *g2)

    own_rows = chunk_rows(0)
    resid = own_tok[...] + summed_relayed(0, rs)
    res_s[...] = resid
    act2[y] = (resid * rms_scale(resid) * gain_two).astype(bf16)
    def act2_slot(i):
        return act2.at[i]

    ag_act2 = ag_y(act2.at[y], act2_slot)
    arrived(ag1)
    arrived(ag2)

    def ffn_part(acts, ups, rows, f_lo, n):
        gu = dot_nn(acts, weights(GU0 + 2 * f_lo, 2 * n))
        gh = dot_nn(ups, weights(DN0 + f_lo, n))
        for j in range(n // 128):
            gate = gu[:, 256 * j : 256 * j + 128]
            up = gu[:, 256 * j + 128 : 256 * j + 256]
            grad = gh[:, 128 * j : 128 * j + 128]
            sig = jax.nn.sigmoid(gate)
            swish = gate * sig
            hidden = (swish * up).astype(bf16)
            grad_gate = (grad * up * sig * (1.0 + gate * (1.0 - sig))).astype(bf16)
            grad_up = (grad * swish).astype(bf16)
            for k, here in enumerate(rows):
                piece = slice(CHUNK * k, CHUNK * k + CHUNK)
                hid[here, pl.ds(f_lo + 128 * j, 128)] = hidden[piece]
                GG[here, pl.ds(2 * f_lo + 256 * j, 128)] = grad_gate[piece]
                GG[here, pl.ds(2 * f_lo + 256 * j + 128, 128)] = grad_up[piece]

    def stacked(parts):
        return parts[0] if len(parts) == 1 else jnp.concatenate(parts, axis=0)

    rs = []
    for steps in ((0,), (1, 3), (2,)):
        if steps == (1, 3):
            ag_act2 = ag_y_pass(ag_act2, act2_slot)
        if steps == (2,):
            arrived(ag_act2)
        rows = [chunk_rows(step) for step in steps]
        acts = stacked([act2[near(y, step)] for step in steps])
        ups = stacked([ulow[here] for here in rows])

        @pl.loop(0, 4)
        def _(t):
            ffn_part(acts, ups, rows, pl.multiple_of(t * 256, 256), 256)

        ffn_part(acts, ups, rows, 1024, 128)
        rs += partial(1, steps, stacked([GG[here] for here in rows]), GU0, 2 * FF)

    def weight_grad(left, right, lo, n):
        for block in range(4):
            values = left(block)
            for start in range(0, n, 256):
                width = min(256, n - start)
                part = dot_tn(values, right[:, pl.ds(start, width)])
                G[block, :, :, :, pl.ds(lo + start, width)] = part.astype(bf16).reshape(
                    4, 2, 32, width
                )

    def rs_core(lo, hi):
        cols = pl.ds(lo, hi - lo)
        return [send(G.at[:, :, oc, :, cols], RC.at[:, :, :, cols], to_core)]

    def rs_one(copies, lo, mid, hi):
        arrived(copies)
        cols = pl.ds(lo, hi - lo)

        @pl.loop(0, 4)
        def _(i):
            for j in range(4):
                G[i, j, c, :, cols] = (
                    G[i, j, c, :, cols].astype(f32) + RC[i, j, :, cols].astype(f32)
                ).astype(bf16)

        a, b = pl.ds(lo, mid - lo), pl.ds(mid, hi - mid)
        out = []
        for s in (1, 3, 2):
            out += [send(G.at[:, near(x, s), c, :, a], RX.at[s - 1, :, :, a], to_x(s))]
            out += [send(G.at[near(z, s), :, c, :, b], RX.at[s - 1, :, :, b], to_z(s))]
        return out

    def rs_two(copies, lo, mid, hi):
        arrived(copies)
        a, b = pl.ds(lo, mid - lo), pl.ds(mid, hi - mid)

        @pl.loop(0, 4)
        def _(i):
            T[i, :, a] = (
                G[i, x, c, :, a].astype(f32)
                + RX[0, i, :, a].astype(f32)
                + RX[1, i, :, a].astype(f32)
                + RX[2, i, :, a].astype(f32)
            ).astype(bf16)
            T[i, :, b] = (
                G[z, i, c, :, b].astype(f32)
                + RX[0, i, :, b].astype(f32)
                + RX[1, i, :, b].astype(f32)
                + RX[2, i, :, b].astype(f32)
            ).astype(bf16)

        out = []
        for s in (1, 3, 2):
            out += [send(T.at[near(z, s), :, a], RZ.at[s - 1, :, a], to_z(s))]
            out += [send(T.at[near(x, s), :, b], RZ.at[s - 1, :, b], to_x(s))]
        return out

    def rs_end(lo, n, mid):
        cols = pl.ds(lo, n)
        mine = z if lo < mid else x
        return (
            T[mine, :, cols].astype(f32)
            + RZ[0, :, cols].astype(f32)
            + RZ[1, :, cols].astype(f32)
            + RZ[2, :, cols].astype(f32)
        )

    gi = (IN0, 512, 1024)
    weight_grad(
        lambda i: act2[:, :, i * 256 : i * 256 + 256].reshape(ROWS, 256), GG, GU0, 2 * FF
    )
    r_gu = rs_core(GU0, DN0)

    back_two = summed(1, rs)
    resid = res_s[...]
    scale_two = rms_scale(resid)
    normed = resid * scale_two
    SM[0] = jnp.zeros((8, D), f32)
    SM[0, 4:5] = jnp.sum(back_two * normed, axis=0, keepdims=True)
    scaled = back_two * gain_two
    grad_resid = cot[own_rows] + scale_two * (
        scaled - normed * jnp.mean(scaled * normed, axis=-1, keepdims=True)
    )
    rlow[y] = grad_resid.astype(bf16)

    def rlow_slot(i):
        return rlow.at[i]

    low_at = counter[0]
    counter[0] += 4
    low_halo = [
        pltpu.make_async_remote_copy(
            rlow.at[0, pl.ds(0, 16)],
            hlow,
            ssem.at[low_at + k],
            rsem.at[low_at],
            device_id=(z, lax.rem(seq + 7, 8), k),
            device_id_type=MESH,
        )
        for k in range(4)
    ]

    @pl.when(y == 0)
    def _():
        for copy in low_halo:
            copy.start()

    ag_rlow = ag_y(rlow.at[y], rlow_slot)
    OWN[1] = grad_resid

    rs_ffn = rs_y(2, hid, DN0, FF)
    r_gu = rs_one(r_gu, *g1)
    ag_rlow = ag_y_pass(ag_rlow, rlow_slot)
    weight_grad(lambda i: ulow[:, i * 256 : i * 256 + 256], hid, DN0, FF)
    r_dn = rs_core(DN0, COLS)
    rs_ffn = rs_y_pass(2, rs_ffn)

    arrived(ag_rlow)

    low = rlow[...].reshape(ROWS, D)
    grad_gated = dot_nn(low, weights(OUT0, CH))
    gext[0:ROWS] = (grad_gated * c_s[...]).astype(bf16).astype(f32)
    low_halo[0].wait_recv()
    after = (dot_nn(hlow[...], weights(OUT0, CH)) * c_after[...]).astype(bf16).astype(f32)
    gext[ROWS : ROWS + 8] = jnp.where(seq < 7, after[0:8], 0.0)
    GB[:, CH : 2 * CH] = (grad_gated * conv_s[...]).astype(bf16)
    grad_mixed = tap2 * gext[0:ROWS] + tap1 * gext[1 : ROWS + 1] + tap0 * gext[2 : ROWS + 2]
    GB[:, 0:CH] = (grad_mixed * x_s[...]).astype(bf16)
    GB[:, 2 * CH : 3 * CH] = (grad_mixed * b_s[...]).astype(bf16)

    rs = rs_y(3, GB, IN0, 3 * CH, tok)
    grad_conv = gext[0:ROWS]
    for k in range(3):
        row = jnp.sum(grad_conv * xext[14 + k : ROWS + 14 + k], axis=0, keepdims=True)
        SM[0, k : k + 1, own_channels] = row
    sm = [send(SM.at[0], SMR.at[0], to_core)]
    weight_grad(
        lambda i: rlow[:, :, i * 256 : i * 256 + 256].reshape(ROWS, 256), gated, GRAD_OUT0, CH
    )
    weight_grad(lambda i: act1[16 : ROWS + 16, i * 256 : i * 256 + 256], GB, IN0, 3 * CH)
    arrived(sm)
    SM[1] = SM[0] + SMR[0]
    sm = [send(SM.at[1], SMR.at[s], to_x(s)) for s in (1, 3, 2)]
    r_in = rs_core(IN0, 1024)
    r_dn = rs_one(r_dn, *g2)
    rs = rs_y_pass(3, rs)

    mixrow[...] = (res_s[...] + summed_relayed(2, rs_ffn)).astype(bf16)

    def mixed_slot(i):
        return mixed_o.at[i]

    ag_mixed = ag_y(mixrow, mixed_slot)
    local_mixed = pltpu.make_async_copy(mixrow, mixed_o.at[y], lsem.at[0])
    local_mixed.start()

    r_in = rs_one(r_in, *gi)

    back_one = summed_relayed(3, rs)
    scale_one = rms_scale(own_tok[...])
    normed = tok[own_rows]
    scaled = back_one * gain_one
    tgrow[...] = (
        OWN[1]
        + scale_one * (scaled - normed * jnp.mean(scaled * normed, axis=-1, keepdims=True))
    ).astype(bf16)

    def tg_slot(i):
        return tg_o.at[i]

    ag_tg = ag_y(tgrow, tg_slot)
    local_tg = pltpu.make_async_copy(tgrow, tg_o.at[y], lsem.at[1])
    local_tg.start()

    arrived(sm)
    SM[2] = SM[1] + SMR[1] + SMR[2] + SMR[3]
    sm = [send(SM.at[2], SMR.at[3 + s], to_z(s)) for s in (1, 3, 2)]
    ag_mixed = ag_y_pass(ag_mixed, mixed_slot)
    r_gu = rs_two(r_gu, *g1)
    r_dn = rs_two(r_dn, *g2)
    arrived(sm)
    SMR[7] = SM[2] + SMR[4] + SMR[5] + SMR[6]
    sm = [send(SMR.at[7], SMR.at[7 + s], to_y(s)) for s in (1, 3, 2)]

    arrived(r_dn)
    g_dn[:, 0:640] = rs_end(DN0, 640, g2[1])
    g_dn[:, 640:1152] = rs_end(DN0 + 640, 512, g2[1])

    r_in = rs_two(r_in, *gi)

    ag_tg = ag_y_pass(ag_tg, tg_slot)
    arrived(r_gu)
    for t in range(9):
        g_gu[0, :, 128 * t : 128 * t + 128] = rs_end(GU0 + 256 * t, 128, g1[1])
        g_gu[1, :, 128 * t : 128 * t + 128] = rs_end(GU0 + 256 * t + 128, 128, g1[1])

    arrived(r_in)
    for k in range(3):
        g_in[k] = rs_end(IN0 + CH * k, CH, gi[1])
    g_out[...] = rs_end(GRAD_OUT0, CH, gi[1])

    arrived(sm)

    def term(j):
        return SMR[7 + lax.rem(y - j + 4, 4)]

    shard_at = z * 8 + seq
    SMR[0] = ((term(0) + term(1)) + term(2)) + term(3)
    four = SMR[0, :, pl.ds(pl.multiple_of(shard_at // 4 * 128, 128), 128)]
    place = lax.rem(shard_at, 4)
    mine = four[:, 0:32]
    for k in range(1, 4):
        mine = jnp.where(place == k, four[:, 32 * k : 32 * k + 32], mine)
    small_o[...] = mine

    arrived(ag_mixed)
    arrived(ag_tg)
    local_mixed.wait()
    local_tg.wait()
    for copy in pending:
        copy.wait_send()

    @pl.when(y == 0)
    def _():
        for copy in low_halo:
            copy.wait_send()


def finish(*refs):
    refs[25][...] = refs[0][...].astype(f32)
    refs[26][...] = refs[1][...].astype(f32)
    small = refs[6][...]
    grads = [ref[...] for ref in refs[2:6]] + [small[0:3], small[3:5]]
    for k, grad in enumerate(grads):
        rate, decay = (rate_matrix, decay_matrix) if k < 4 else (rate_small, 0.0)
        group = refs[7 + 3 * k : 10 + 3 * k]
        new = adamw(*(ref[...] for ref in group), grad, rate, decay)
        for ref, value in zip(refs[27 + 3 * k : 30 + 3 * k], new):
            ref[...] = value


def local(
    tokens,
    cotangent,
    in_weight,
    in_first,
    in_second,
    out_weight,
    out_first,
    out_second,
    gu_weight,
    gu_first,
    gu_second,
    down_weight,
    down_first,
    down_second,
    conv_weight,
    conv_first,
    conv_second,
    norm_gains,
    gains_first,
    gains_second,
):
    vmem = pl.BlockSpec(memory_space=pltpu.VMEM)
    hbm = pl.BlockSpec(memory_space=pl.ANY)
    shape = jax.ShapeDtypeStruct
    mixed, tg, grad_in, grad_out, grad_gu, grad_dn, grad_small = pl.pallas_call(
        kernel,
        out_shape=(
            shape((4, CHUNK, D), bf16),
            shape((4, CHUNK, D), bf16),
            shape((3, 32, CH), f32),
            shape((32, CH), f32),
            shape((2, 32, FF), f32),
            shape((32, FF), f32),
            shape((8, 32), f32),
        ),
        in_specs=[hbm] * 2 + [vmem] * 6,
        out_specs=(hbm, hbm, vmem, vmem, vmem, vmem, vmem),
        scratch_shapes=[
            pltpu.VMEM((ROWS, D), f32),
            pltpu.VMEM((ROWS, D), f32),
            pltpu.VMEM((2, 16, D), f32),
            pltpu.VMEM((128, 128), f32),
            pltpu.VMEM((4, 4, 2, 32, COLS), bf16),
            pltpu.VMEM((4, 4, 2, 32, COLS), bf16),
            pltpu.VMEM((4, 4, 32, COLS), bf16),
            pltpu.VMEM((3, 4, 32, COLS), bf16),
            pltpu.VMEM((4, 32, COLS), bf16),
            pltpu.VMEM((3, 32, COLS), bf16),
            pltpu.VMEM((ROWS + 32, D), bf16),
            pltpu.VMEM((ROWS, D), bf16),
            pltpu.VMEM((4, CHUNK, D), bf16),
            pltpu.VMEM((4, CHUNK, D), bf16),
            pltpu.VMEM((ROWS, FF), bf16),
            pltpu.VMEM((ROWS, 2 * FF), bf16),
            pltpu.VMEM((ROWS, CH), f32),
            pltpu.VMEM((ROWS, CH), f32),
            pltpu.VMEM((ROWS, CH), f32),
            pltpu.VMEM((ROWS, CH), f32),
            pltpu.VMEM((ROWS + 16, CH), f32),
            pltpu.VMEM((ROWS + 8, CH), f32),
            pltpu.VMEM((16, D), bf16),
            pltpu.VMEM((ROWS, CH), bf16),
            pltpu.VMEM((ROWS, 3 * CH), bf16),
            pltpu.VMEM((16, CH), f32),
            pltpu.VMEM((8, D), f32),
            pltpu.VMEM((3, 8, D), f32),
            pltpu.VMEM((11, 8, D), f32),
            pltpu.VMEM((4, 3, CHUNK, D), bf16),
            pltpu.VMEM((4, 3, CHUNK, D), bf16),
            pltpu.VMEM((4, CHUNK, D), f32),
            pltpu.VMEM((CHUNK, D), f32),
            pltpu.VMEM((CHUNK, D), f32),
            pltpu.VMEM((CHUNK, D), bf16),
            pltpu.VMEM((CHUNK, D), bf16),
            pltpu.SemaphoreType.DMA((N_SEMS,)),
            pltpu.SemaphoreType.DMA((N_SEMS,)),
            pltpu.SemaphoreType.DMA((4,)),
        ],
        name="block_step",
        compiler_params=pltpu.CompilerParams(
            collective_id=0, has_side_effects=True, vmem_limit_bytes=62 << 20
        ),
    )(
        tokens.reshape(ROWS, D),
        cotangent.reshape(ROWS, D),
        in_weight,
        out_weight.T,
        gu_weight,
        down_weight.T,
        conv_weight,
        norm_gains,
    )
    params = (
        (in_weight, in_first, in_second),
        (out_weight.T, out_first.T, out_second.T),
        (gu_weight, gu_first, gu_second),
        (down_weight.T, down_first.T, down_second.T),
        (conv_weight, conv_first, conv_second),
        (norm_gains, gains_first, gains_second),
    )
    grads = (grad_in, grad_out, grad_gu, grad_dn, grad_small)
    big = pl.BlockSpec((CHUNK, D), lambda i: (i, 0))

    def rows_of(array):
        if array.ndim == 3:
            return pl.BlockSpec((array.shape[0], 8, array.shape[2]), lambda i: (0, i, 0))
        if array.shape[0] == 32:
            return pl.BlockSpec((8, array.shape[1]), lambda i: (i, 0))
        return pl.BlockSpec(array.shape, lambda i: (0, 0))

    flat_params = [array for group in params for array in group]
    specs = [rows_of(array) for array in flat_params]
    done = pl.pallas_call(
        finish,
        grid=(4,),
        out_shape=[shape((ROWS, D), f32)] * 2 + [shape(v.shape, f32) for v in flat_params],
        in_specs=[big, big] + [rows_of(v) for v in grads] + specs,
        out_specs=[big, big] + specs,
        name="finish",
    )(mixed.reshape(ROWS, D), tg.reshape(ROWS, D), *grads, *flat_params)
    news = [done[2 + 3 * k : 5 + 3 * k] for k in range(6)]
    return (
        done[0].reshape(tokens.shape),
        done[1].reshape(tokens.shape),
        *news[0],
        *(v.T for v in news[1]),
        *news[2],
        *(v.T for v in news[3]),
        *news[4],
        *news[5],
    )


def solution(mesh):
    rows = P("dp", "seq", None)
    stack = P(None, ("dp", "seq"), "mp")
    flat = P("mp", ("dp", "seq"))
    thin = P(None, ("dp", "seq"))
    groups = (stack,) * 3 + (flat,) * 3 + (stack,) * 3 + (flat,) * 3 + (thin,) * 6
    return jax.shard_map(
        local,
        mesh=mesh,
        in_specs=(rows, rows) + groups,
        out_specs=(rows, rows) + groups,
        check_vma=False,
    )
```

```python
import jax
import jax.numpy as jnp
from jax import lax
from jax.experimental import pallas as pl
from jax.experimental.pallas import tpu as pltpu
from jax.sharding import PartitionSpec as P

STEP = 10

beta_one = 0.9
beta_two = 0.95
eps_adam = 1e-08
eps_norm = 1e-05
rate_matrix = 0.05
rate_small = 0.3
decay_matrix = 0.1

MESH = pl.DeviceIdType.MESH
bf16 = jnp.bfloat16
f32 = jnp.float32

ROWS = 512
CHUNK = 128
D = 1024
CH = 256
FF = 1152
IN0, SM0, OUT0, GU0, DN0, COLS = 0, 768, 896, 1152, 3456, 4608
GRAD_OUT0 = 768


def adamw(master, first, second, grad, rate, decay):
    moment = beta_one * first + (1.0 - beta_one) * grad
    square = beta_two * second + (1.0 - beta_two) * grad * grad
    moment_hat = moment / (1.0 - beta_one**STEP)
    square_hat = square / (1.0 - beta_two**STEP)
    renewed = master - rate * (moment_hat / (jnp.sqrt(square_hat) + eps_adam) + decay * master)
    return (renewed, moment, square)


def rms_scale(values):
    return lax.rsqrt(jnp.mean(values * values, axis=-1, keepdims=True) + eps_norm)


def dot_nn(a, b):
    return jnp.dot(a, b, preferred_element_type=f32)


def dot_nt(a, b):
    return lax.dot_general(a, b, (((1,), (1,)), ((), ())), preferred_element_type=f32)


def dot_tn(a, b):
    return lax.dot_general(a, b, (((0,), (0,)), ((), ())), preferred_element_type=f32)


N_SEMS = 192


def kernel(
    tok_h,
    cot_h,
    w_in,
    w_out,
    w_gu,
    w_dn,
    w_conv,
    w_gain,
    mixed_o,
    tg_o,
    g_in,
    g_out,
    g_gu,
    g_dn,
    small_o,
    tok,
    cot,
    htok,
    square,
    W,
    G,
    RC,
    RX,
    T,
    RZ,
    act1,
    ulow,
    act2,
    rlow,
    hid,
    GG,
    b_s,
    c_s,
    x_s,
    conv_s,
    xext,
    gext,
    hlow,
    gated,
    GB,
    c_after,
    smw,
    SM,
    SMR,
    PY,
    RY,
    OWN,
    res_s,
    own_tok,
    mixrow,
    tgrow,
    ssem,
    rsem,
    lsem,
):
    z = lax.axis_index("dp")
    seq = lax.axis_index("seq")
    y = lax.axis_index("mp")
    x = seq // 2
    c = lax.rem(seq, 2)
    oc = 1 - c

    def near(value, step):
        return lax.rem(value + step, 4)

    def to_x(step):
        return (z, near(x, step) * 2 + c, y)

    def to_z(step):
        return (near(z, step), seq, y)

    def to_y(step):
        return (z, seq, near(y, step))

    to_core = (z, x * 2 + oc, y)
    to_next = (z, lax.rem(seq + 1, 8), y)
    to_prev = (z, lax.rem(seq + 7, 8), y)

    counter = [0]
    pending = []

    def send(src, dst, where):
        i = counter[0]
        assert i < N_SEMS
        counter[0] += 1
        copy = pltpu.make_async_remote_copy(
            src, dst, ssem.at[i], rsem.at[i], device_id=where, device_id_type=MESH
        )
        copy.start()
        pending.append(copy)
        return copy

    def arrived(copies):
        for copy in copies:
            copy.wait_recv()

    barrier = pltpu.get_barrier_semaphore()
    peers = [to_core, to_prev] + [(z, lax.rem(seq + 1, 8), k) for k in range(4)]
    for step in (1, 2, 3):
        peers += [to_x(step), to_z(step), to_y(step)]
    for peer in peers:
        pl.semaphore_signal(barrier, inc=1, device_id=peer, device_id_type=MESH)
    load_tok = pltpu.make_async_copy(tok_h, tok, lsem.at[2])
    load_tok.start()
    load_cot = pltpu.make_async_copy(cot_h, cot, lsem.at[3])
    load_cot.start()

    for k in range(3):
        W[z, x, c, :, CH * k : CH * k + CH] = w_in[k].astype(bf16)
    W[z, x, c, :, OUT0:GU0] = w_out[...].astype(bf16)
    square[...] = jnp.zeros((128, 128), f32)
    square[0:3, 0:32] = w_conv[...]
    square[3:5, 0:32] = w_gain[...]
    W[z, x, c, :, SM0:OUT0] = square[...].T[0:32].astype(bf16)
    pl.semaphore_wait(barrier, len(peers))

    def ag_one(lo, mid, hi):
        a, b = pl.ds(lo, mid - lo), pl.ds(mid, hi - mid)
        src_a, src_b = W.at[z, x, c, :, a], W.at[z, x, c, :, b]
        return (
            [send(src_a, src_a, to_x(s)) for s in (1, 3, 2)],
            [send(src_b, src_b, to_z(s)) for s in (1, 3, 2)],
        )

    def ag_two(copies, lo, mid, hi):
        a, b = pl.ds(lo, mid - lo), pl.ds(mid, hi - mid)
        src_a, src_b = W.at[z, :, c, :, a], W.at[:, x, c, :, b]
        arrived(copies[0])
        first = [send(src_a, src_a, to_z(s)) for s in (1, 3)]
        arrived(copies[1])
        second = [send(src_b, src_b, to_x(s)) for s in (1, 3)]
        return first, second, [send(src_a, src_a, to_core), send(src_b, src_b, to_core)]

    def ag_pass(copies, lo, mid, hi):
        core = copies[2]
        a, b = pl.ds(lo, mid - lo), pl.ds(mid, hi - mid)
        low, high = pl.ds(0, 2), pl.ds(2, 2)
        out = []
        for s, half in ((1, low), (3, high)):
            i = 0 if s == 1 else 1
            arrived([copies[0][i]])
            src = W.at[near(z, 4 - s), half, c, :, a]
            out += [send(src, src, to_z(s))]
            arrived([copies[1][i]])
            src = W.at[half, near(x, 4 - s), c, :, b]
            out += [send(src, src, to_x(s))]
            src = W.at[near(z, 4 - s), :, c, :, a]
            core = core + [send(src, src, to_core)]
            src = W.at[:, near(x, 4 - s), c, :, b]
            core = core + [send(src, src, to_core)]
        return out, core

    def ag_three(copies, lo, mid, hi):
        a, b = pl.ds(lo, mid - lo), pl.ds(mid, hi - mid)
        arrived(copies[0])
        src_a, src_b = W.at[near(z, 2), :, c, :, a], W.at[:, near(x, 2), c, :, b]
        return copies[1] + [send(src_a, src_a, to_core), send(src_b, src_b, to_core)]

    def ag_two_direct(copies, lo, mid, hi):
        a, b = pl.ds(lo, mid - lo), pl.ds(mid, hi - mid)
        src_a, src_b = W.at[z, :, c, :, a], W.at[:, x, c, :, b]
        arrived(copies[0])
        first = [send(src_a, src_a, to_z(s)) for s in (1, 3, 2)]
        arrived(copies[1])
        second = [send(src_b, src_b, to_x(s)) for s in (1, 3, 2)]
        core = [send(src_a, src_a, to_core), send(src_b, src_b, to_core)]
        return first, second, core

    def ag_three_direct(copies, lo, mid, hi):
        a, b = pl.ds(lo, mid - lo), pl.ds(mid, hi - mid)
        first, second, core = copies
        for k, s in enumerate((1, 3, 2)):
            arrived([first[k]])
            src = W.at[near(z, 4 - s), :, c, :, a]
            core = core + [send(src, src, to_core)]
            arrived([second[k]])
            src = W.at[:, near(x, 4 - s), c, :, b]
            core = core + [send(src, src, to_core)]
        return core

    g0 = (IN0, 512, OUT0)
    go = (OUT0, OUT0 + 128, GU0)
    g1 = (GU0, GU0 + 1152, DN0)
    g2 = (DN0, DN0 + 640, COLS)
    ag0 = ag_one(*g0)
    ago = ag_one(*go)
    halo = [
        send(tok_h.at[pl.ds(ROWS - 16, 16)], htok.at[0], to_next),
        send(tok_h.at[pl.ds(0, 16)], htok.at[1], to_prev),
    ]
    for t in range(9):
        for k in range(2):
            at = GU0 + 256 * t + 128 * k
            W[z, x, c, :, at : at + 128] = w_gu[k, :, 128 * t : 128 * t + 128].astype(bf16)
    W[z, x, c, :, DN0:COLS] = w_dn[...].astype(bf16)
    ag0 = ag_two_direct(ag0, *g0)
    ago = ag_two_direct(ago, *go)
    ag1 = ag_one(*g1)
    ag2 = ag_one(*g2)
    load_tok.wait()
    mine = pl.ds(pl.multiple_of(y * CHUNK, CHUNK), CHUNK)
    own_tok[...] = tok[mine]
    for i in range(4):
        here = slice(CHUNK * i, CHUNK * i + CHUNK)
        v = tok[here]
        tok[here] = v * rms_scale(v)
    ag0 = ag_three_direct(ag0, *g0)
    ag1 = ag_two(ag1, *g1)
    ag2 = ag_two(ag2, *g2)
    load_cot.wait()
    for r in range(0, ROWS, 128):
        ulow[r : r + 128] = cot[r : r + 128].astype(bf16)
    ago = ag_three_direct(ago, *go)
    arrived(ag0)

    def weights(lo, n):
        return W[:, :, :, :, pl.ds(lo, n)].reshape(D, n)

    def weight_rows(block, lo, n):
        return W[block, :, :, :, pl.ds(lo, n)].reshape(256, n)

    smw[...] = weights(SM0, 128).astype(f32).T[:8]
    gain_one = smw[3:4]
    gain_two = smw[4:5]
    own_channels = pl.ds(pl.multiple_of(y * CH, CH), CH)
    taps = smw[:, own_channels]
    tap0, tap1, tap2 = taps[0:1], taps[1:2], taps[2:3]

    for i in range(4):
        act1[CHUNK * i + 16 : CHUNK * i + 144] = (tok[CHUNK * i : CHUNK * i + CHUNK] * gain_one).astype(bf16)
    arrived(halo)
    for i in range(2):
        v = htok[i]
        at = i * (ROWS + 16)
        act1[at : at + 16] = (v * rms_scale(v) * gain_one).astype(bf16)
    bgate = dot_nn(act1[0 : ROWS + 16], weights(0, CH))
    xvalue = dot_nn(act1[0 : ROWS + 16], weights(2 * CH, CH))
    xext[...] = (bgate * xvalue).astype(bf16).astype(f32)
    b_s[...] = bgate[16:]
    x_s[...] = xvalue[16:]
    xext[0:16] = jnp.where(seq > 0, xext[0:16], 0.0)
    cgate = dot_nn(act1[16:], weights(CH, CH))
    c_s[...] = cgate[0:ROWS]
    c_after[...] = cgate[ROWS:]
    conv_s[...] = (
        tap0 * xext[14 : ROWS + 14] + tap1 * xext[15 : ROWS + 15] + tap2 * xext[16 : ROWS + 16]
    )
    gated[...] = (c_s[...] * conv_s[...]).astype(bf16)
    arrived(ago)

    def chunk_rows(step):
        return pl.ds(pl.multiple_of(near(y, step) * CHUNK, CHUNK), CHUNK)

    def partial(which, steps, values, lo, n):
        for block in range(4):
            part = dot_nt(values, weight_rows(block, lo, n))
            cols = slice(block * 256, block * 256 + 256)
            for k, step in enumerate(steps):
                piece = part[CHUNK * k : CHUNK * k + CHUNK]
                if step == 0:
                    OWN[which, :, cols] = piece
                else:
                    PY[which, step - 1, :, cols] = piece.astype(bf16)
        return [
            send(PY.at[which, step - 1], RY.at[which, step - 1], to_y(step))
            for step in steps
            if step
        ]

    half = CHUNK // 2
    low_half, high_half = pl.ds(0, half), pl.ds(half, half)

    def part_of(which, slot, rows, where):
        return send(PY.at[which, slot, rows], RY.at[which, slot, rows], where)

    def rs_y(which, source, lo, n, against=None):
        def block_of(step):
            return source[chunk_rows(step)]

        for step in (2, 1, 3, 0):
            values = block_of(step)
            for block in range(4):
                part = dot_nt(values, weight_rows(block, lo, n))
                cols = slice(block * 256, block * 256 + 256)
                if against is not None:
                    SM[0, 3:4, cols] += jnp.sum(
                        part * against[chunk_rows(step), cols], axis=0, keepdims=True
                    )
                if step == 0:
                    OWN[which, :, cols] = part
                else:
                    PY[which, step - 1, :, cols] = part.astype(bf16)
            if step == 2:
                relay = (
                    part_of(which, 1, low_half, to_y(1)),
                    part_of(which, 1, high_half, to_y(3)),
                )
            elif step == 1:
                direct = [part_of(which, 0, high_half, to_y(1))]
            elif step == 3:
                direct += [part_of(which, 2, low_half, to_y(3))]
        return relay, direct

    def rs_y_pass(which, state):
        relay, direct = state
        out = list(direct)
        for k, (slot, rows, where) in enumerate(
            ((0, slice(0, half), to_y(1)), (2, slice(half, CHUNK), to_y(3)))
        ):
            arrived([relay[k]])
            PY[which, slot, rows] = (
                PY[which, slot, rows].astype(f32) + RY[which, 1, rows].astype(f32)
            ).astype(bf16)
            out += [part_of(which, slot, low_half if k == 0 else high_half, where)]
        return out

    def summed_relayed(which, copies):
        arrived(copies)
        return OWN[which] + RY[which, 0].astype(f32) + RY[which, 2].astype(f32)

    def summed(which, copies):
        arrived(copies)
        return (
            OWN[which]
            + RY[which, 0].astype(f32)
            + RY[which, 1].astype(f32)
            + RY[which, 2].astype(f32)
        )

    def ag_y(src, slot):
        return (send(src, slot(y), to_y(1)), send(src, slot(y), to_y(3)))

    def ag_y_pass(copies, slot):
        arrived(copies[:1])
        left = slot(near(y, 3)).at[pl.ds(0, half)]
        out = [send(left, left, to_y(1))]
        arrived(copies[1:])
        right = slot(near(y, 1)).at[pl.ds(half, half)]
        return out + [send(right, right, to_y(3))]

    rs = rs_y(0, gated, OUT0, CH)
    ag1 = ag_pass(ag1, *g1)
    ag2 = ag_pass(ag2, *g2)
    rs = rs_y_pass(0, rs)
    ag1 = ag_three(ag1, *g1)
    ag2 = ag_three(ag2, *g2)

    own_rows = chunk_rows(0)
    resid = own_tok[...] + summed_relayed(0, rs)
    res_s[...] = resid
    act2[y] = (resid * rms_scale(resid) * gain_two).astype(bf16)
    def act2_slot(i):
        return act2.at[i]

    ag_act2 = ag_y(act2.at[y], act2_slot)
    arrived(ag1)
    arrived(ag2)

    def ffn_part(acts, ups, rows, f_lo, n):
        gu = dot_nn(acts, weights(GU0 + 2 * f_lo, 2 * n))
        gh = dot_nn(ups, weights(DN0 + f_lo, n))
        for j in range(n // 128):
            gate = gu[:, 256 * j : 256 * j + 128]
            up = gu[:, 256 * j + 128 : 256 * j + 256]
            grad = gh[:, 128 * j : 128 * j + 128]
            sig = jax.nn.sigmoid(gate)
            swish = gate * sig
            hidden = (swish * up).astype(bf16)
            grad_gate = (grad * up * sig * (1.0 + gate * (1.0 - sig))).astype(bf16)
            grad_up = (grad * swish).astype(bf16)
            for k, here in enumerate(rows):
                piece = slice(CHUNK * k, CHUNK * k + CHUNK)
                hid[here, pl.ds(f_lo + 128 * j, 128)] = hidden[piece]
                GG[here, pl.ds(2 * f_lo + 256 * j, 128)] = grad_gate[piece]
                GG[here, pl.ds(2 * f_lo + 256 * j + 128, 128)] = grad_up[piece]

    def stacked(parts):
        return parts[0] if len(parts) == 1 else jnp.concatenate(parts, axis=0)

    rs = []
    for steps in ((0,), (1, 3), (2,)):
        if steps == (1, 3):
            ag_act2 = ag_y_pass(ag_act2, act2_slot)
        if steps == (2,):
            arrived(ag_act2)
        rows = [chunk_rows(step) for step in steps]
        acts = stacked([act2[near(y, step)] for step in steps])
        ups = stacked([ulow[here] for here in rows])

        @pl.loop(0, 4)
        def _(t):
            ffn_part(acts, ups, rows, pl.multiple_of(t * 256, 256), 256)

        ffn_part(acts, ups, rows, 1024, 128)
        rs += partial(1, steps, stacked([GG[here] for here in rows]), GU0, 2 * FF)

    def weight_grad(left, right, lo, n):
        for block in range(4):
            values = left(block)
            for start in range(0, n, 256):
                width = min(256, n - start)
                part = dot_tn(values, right[:, pl.ds(start, width)])
                G[block, :, :, :, pl.ds(lo + start, width)] = part.astype(bf16).reshape(
                    4, 2, 32, width
                )

    def rs_core(lo, hi):
        cols = pl.ds(lo, hi - lo)
        return [send(G.at[:, :, oc, :, cols], RC.at[:, :, :, cols], to_core)]

    def rs_one(copies, lo, mid, hi):
        arrived(copies)
        cols = pl.ds(lo, hi - lo)

        @pl.loop(0, 4)
        def _(i):
            for j in range(4):
                G[i, j, c, :, cols] = (
                    G[i, j, c, :, cols].astype(f32) + RC[i, j, :, cols].astype(f32)
                ).astype(bf16)

        a, b = pl.ds(lo, mid - lo), pl.ds(mid, hi - mid)
        out = []
        for s in (1, 3, 2):
            out += [send(G.at[:, near(x, s), c, :, a], RX.at[s - 1, :, :, a], to_x(s))]
            out += [send(G.at[near(z, s), :, c, :, b], RX.at[s - 1, :, :, b], to_z(s))]
        return out

    def rs_two(copies, lo, mid, hi):
        arrived(copies)
        a, b = pl.ds(lo, mid - lo), pl.ds(mid, hi - mid)

        @pl.loop(0, 4)
        def _(i):
            T[i, :, a] = (
                G[i, x, c, :, a].astype(f32)
                + RX[0, i, :, a].astype(f32)
                + RX[1, i, :, a].astype(f32)
                + RX[2, i, :, a].astype(f32)
            ).astype(bf16)
            T[i, :, b] = (
                G[z, i, c, :, b].astype(f32)
                + RX[0, i, :, b].astype(f32)
                + RX[1, i, :, b].astype(f32)
                + RX[2, i, :, b].astype(f32)
            ).astype(bf16)

        out = []
        for s in (1, 3, 2):
            out += [send(T.at[near(z, s), :, a], RZ.at[s - 1, :, a], to_z(s))]
            out += [send(T.at[near(x, s), :, b], RZ.at[s - 1, :, b], to_x(s))]
        return out

    def rs_end(lo, n, mid):
        cols = pl.ds(lo, n)
        mine = z if lo < mid else x
        return (
            T[mine, :, cols].astype(f32)
            + RZ[0, :, cols].astype(f32)
            + RZ[1, :, cols].astype(f32)
            + RZ[2, :, cols].astype(f32)
        )

    gi = (IN0, 512, 1024)
    weight_grad(
        lambda i: act2[:, :, i * 256 : i * 256 + 256].reshape(ROWS, 256), GG, GU0, 2 * FF
    )
    r_gu = rs_core(GU0, DN0)

    back_two = summed(1, rs)
    resid = res_s[...]
    scale_two = rms_scale(resid)
    normed = resid * scale_two
    SM[0] = jnp.zeros((8, D), f32)
    SM[0, 4:5] = jnp.sum(back_two * normed, axis=0, keepdims=True)
    scaled = back_two * gain_two
    grad_resid = cot[own_rows] + scale_two * (
        scaled - normed * jnp.mean(scaled * normed, axis=-1, keepdims=True)
    )
    rlow[y] = grad_resid.astype(bf16)

    def rlow_slot(i):
        return rlow.at[i]

    low_at = counter[0]
    counter[0] += 4
    low_halo = [
        pltpu.make_async_remote_copy(
            rlow.at[0, pl.ds(0, 16)],
            hlow,
            ssem.at[low_at + k],
            rsem.at[low_at],
            device_id=(z, lax.rem(seq + 7, 8), k),
            device_id_type=MESH,
        )
        for k in range(4)
    ]

    @pl.when(y == 0)
    def _():
        for copy in low_halo:
            copy.start()

    ag_rlow = ag_y(rlow.at[y], rlow_slot)
    OWN[1] = grad_resid

    rs_ffn = rs_y(2, hid, DN0, FF)
    r_gu = rs_one(r_gu, *g1)
    ag_rlow = ag_y_pass(ag_rlow, rlow_slot)
    weight_grad(lambda i: ulow[:, i * 256 : i * 256 + 256], hid, DN0, FF)
    r_dn = rs_core(DN0, COLS)
    rs_ffn = rs_y_pass(2, rs_ffn)

    arrived(ag_rlow)

    r_dn = rs_one(r_dn, *g2)

    low = rlow[...].reshape(ROWS, D)
    grad_gated = dot_nn(low, weights(OUT0, CH))
    gext[0:ROWS] = (grad_gated * c_s[...]).astype(bf16).astype(f32)
    low_halo[0].wait_recv()
    after = (dot_nn(hlow[...], weights(OUT0, CH)) * c_after[...]).astype(bf16).astype(f32)
    gext[ROWS : ROWS + 8] = jnp.where(seq < 7, after[0:8], 0.0)
    GB[:, CH : 2 * CH] = (grad_gated * conv_s[...]).astype(bf16)
    grad_mixed = tap2 * gext[0:ROWS] + tap1 * gext[1 : ROWS + 1] + tap0 * gext[2 : ROWS + 2]
    GB[:, 0:CH] = (grad_mixed * x_s[...]).astype(bf16)
    GB[:, 2 * CH : 3 * CH] = (grad_mixed * b_s[...]).astype(bf16)

    rs = rs_y(3, GB, IN0, 3 * CH, tok)
    grad_conv = gext[0:ROWS]
    for k in range(3):
        row = jnp.sum(grad_conv * xext[14 + k : ROWS + 14 + k], axis=0, keepdims=True)
        SM[0, k : k + 1, own_channels] = row
    sm = [send(SM.at[0], SMR.at[0], to_core)]
    weight_grad(
        lambda i: rlow[:, :, i * 256 : i * 256 + 256].reshape(ROWS, 256), gated, GRAD_OUT0, CH
    )
    weight_grad(lambda i: act1[16 : ROWS + 16, i * 256 : i * 256 + 256], GB, IN0, 3 * CH)
    arrived(sm)
    SM[1] = SM[0] + SMR[0]
    sm = [send(SM.at[1], SMR.at[s], to_x(s)) for s in (1, 3, 2)]
    r_in = rs_core(IN0, 1024)
    rs = rs_y_pass(3, rs)

    mixrow[...] = (res_s[...] + summed_relayed(2, rs_ffn)).astype(bf16)

    def mixed_slot(i):
        return mixed_o.at[i]

    ag_mixed = ag_y(mixrow, mixed_slot)
    local_mixed = pltpu.make_async_copy(mixrow, mixed_o.at[y], lsem.at[0])
    local_mixed.start()

    r_in = rs_one(r_in, *gi)

    back_one = summed_relayed(3, rs)
    scale_one = rms_scale(own_tok[...])
    normed = tok[own_rows]
    scaled = back_one * gain_one
    tgrow[...] = (
        OWN[1]
        + scale_one * (scaled - normed * jnp.mean(scaled * normed, axis=-1, keepdims=True))
    ).astype(bf16)

    def tg_slot(i):
        return tg_o.at[i]

    ag_tg = ag_y(tgrow, tg_slot)
    local_tg = pltpu.make_async_copy(tgrow, tg_o.at[y], lsem.at[1])
    local_tg.start()

    arrived(sm)
    SM[2] = SM[1] + SMR[1] + SMR[2] + SMR[3]
    sm = [send(SM.at[2], SMR.at[3 + s], to_z(s)) for s in (1, 3, 2)]
    ag_mixed = ag_y_pass(ag_mixed, mixed_slot)
    r_gu = rs_two(r_gu, *g1)
    r_dn = rs_two(r_dn, *g2)
    arrived(sm)
    SMR[7] = SM[2] + SMR[4] + SMR[5] + SMR[6]
    sm = [send(SMR.at[7], SMR.at[7 + s], to_y(s)) for s in (1, 3, 2)]

    arrived(r_dn)
    g_dn[:, 0:640] = rs_end(DN0, 640, g2[1])
    g_dn[:, 640:1152] = rs_end(DN0 + 640, 512, g2[1])

    r_in = rs_two(r_in, *gi)

    ag_tg = ag_y_pass(ag_tg, tg_slot)
    arrived(r_gu)
    for t in range(9):
        g_gu[0, :, 128 * t : 128 * t + 128] = rs_end(GU0 + 256 * t, 128, g1[1])
        g_gu[1, :, 128 * t : 128 * t + 128] = rs_end(GU0 + 256 * t + 128, 128, g1[1])

    arrived(r_in)
    for k in range(3):
        g_in[k] = rs_end(IN0 + CH * k, CH, gi[1])
    g_out[...] = rs_end(GRAD_OUT0, CH, gi[1])

    arrived(sm)

    def term(j):
        return SMR[7 + lax.rem(y - j + 4, 4)]

    shard_at = z * 8 + seq
    SMR[0] = ((term(0) + term(1)) + term(2)) + term(3)
    four = SMR[0, :, pl.ds(pl.multiple_of(shard_at // 4 * 128, 128), 128)]
    place = lax.rem(shard_at, 4)
    mine = four[:, 0:32]
    for k in range(1, 4):
        mine = jnp.where(place == k, four[:, 32 * k : 32 * k + 32], mine)
    small_o[...] = mine

    arrived(ag_mixed)
    arrived(ag_tg)
    local_mixed.wait()
    local_tg.wait()
    for copy in pending:
        copy.wait_send()

    @pl.when(y == 0)
    def _():
        for copy in low_halo:
            copy.wait_send()


def finish(*refs):
    refs[25][...] = refs[0][...].astype(f32)
    refs[26][...] = refs[1][...].astype(f32)
    small = refs[6][...]
    grads = [ref[...] for ref in refs[2:6]] + [small[0:3], small[3:5]]
    for k, grad in enumerate(grads):
        rate, decay = (rate_matrix, decay_matrix) if k < 4 else (rate_small, 0.0)
        group = refs[7 + 3 * k : 10 + 3 * k]
        new = adamw(*(ref[...] for ref in group), grad, rate, decay)
        for ref, value in zip(refs[27 + 3 * k : 30 + 3 * k], new):
            ref[...] = value


def local(
    tokens,
    cotangent,
    in_weight,
    in_first,
    in_second,
    out_weight,
    out_first,
    out_second,
    gu_weight,
    gu_first,
    gu_second,
    down_weight,
    down_first,
    down_second,
    conv_weight,
    conv_first,
    conv_second,
    norm_gains,
    gains_first,
    gains_second,
):
    vmem = pl.BlockSpec(memory_space=pltpu.VMEM)
    hbm = pl.BlockSpec(memory_space=pl.ANY)
    shape = jax.ShapeDtypeStruct
    mixed, tg, grad_in, grad_out, grad_gu, grad_dn, grad_small = pl.pallas_call(
        kernel,
        out_shape=(
            shape((4, CHUNK, D), bf16),
            shape((4, CHUNK, D), bf16),
            shape((3, 32, CH), f32),
            shape((32, CH), f32),
            shape((2, 32, FF), f32),
            shape((32, FF), f32),
            shape((8, 32), f32),
        ),
        in_specs=[hbm] * 2 + [vmem] * 6,
        out_specs=(hbm, hbm, vmem, vmem, vmem, vmem, vmem),
        scratch_shapes=[
            pltpu.VMEM((ROWS, D), f32),
            pltpu.VMEM((ROWS, D), f32),
            pltpu.VMEM((2, 16, D), f32),
            pltpu.VMEM((128, 128), f32),
            pltpu.VMEM((4, 4, 2, 32, COLS), bf16),
            pltpu.VMEM((4, 4, 2, 32, COLS), bf16),
            pltpu.VMEM((4, 4, 32, COLS), bf16),
            pltpu.VMEM((3, 4, 32, COLS), bf16),
            pltpu.VMEM((4, 32, COLS), bf16),
            pltpu.VMEM((3, 32, COLS), bf16),
            pltpu.VMEM((ROWS + 32, D), bf16),
            pltpu.VMEM((ROWS, D), bf16),
            pltpu.VMEM((4, CHUNK, D), bf16),
            pltpu.VMEM((4, CHUNK, D), bf16),
            pltpu.VMEM((ROWS, FF), bf16),
            pltpu.VMEM((ROWS, 2 * FF), bf16),
            pltpu.VMEM((ROWS, CH), f32),
            pltpu.VMEM((ROWS, CH), f32),
            pltpu.VMEM((ROWS, CH), f32),
            pltpu.VMEM((ROWS, CH), f32),
            pltpu.VMEM((ROWS + 16, CH), f32),
            pltpu.VMEM((ROWS + 8, CH), f32),
            pltpu.VMEM((16, D), bf16),
            pltpu.VMEM((ROWS, CH), bf16),
            pltpu.VMEM((ROWS, 3 * CH), bf16),
            pltpu.VMEM((16, CH), f32),
            pltpu.VMEM((8, D), f32),
            pltpu.VMEM((3, 8, D), f32),
            pltpu.VMEM((11, 8, D), f32),
            pltpu.VMEM((4, 3, CHUNK, D), bf16),
            pltpu.VMEM((4, 3, CHUNK, D), bf16),
            pltpu.VMEM((4, CHUNK, D), f32),
            pltpu.VMEM((CHUNK, D), f32),
            pltpu.VMEM((CHUNK, D), f32),
            pltpu.VMEM((CHUNK, D), bf16),
            pltpu.VMEM((CHUNK, D), bf16),
            pltpu.SemaphoreType.DMA((N_SEMS,)),
            pltpu.SemaphoreType.DMA((N_SEMS,)),
            pltpu.SemaphoreType.DMA((4,)),
        ],
        name="block_step",
        compiler_params=pltpu.CompilerParams(
            collective_id=0, has_side_effects=True, vmem_limit_bytes=62 << 20
        ),
    )(
        tokens.reshape(ROWS, D),
        cotangent.reshape(ROWS, D),
        in_weight,
        out_weight.T,
        gu_weight,
        down_weight.T,
        conv_weight,
        norm_gains,
    )
    params = (
        (in_weight, in_first, in_second),
        (out_weight.T, out_first.T, out_second.T),
        (gu_weight, gu_first, gu_second),
        (down_weight.T, down_first.T, down_second.T),
        (conv_weight, conv_first, conv_second),
        (norm_gains, gains_first, gains_second),
    )
    grads = (grad_in, grad_out, grad_gu, grad_dn, grad_small)
    big = pl.BlockSpec((CHUNK, D), lambda i: (i, 0))

    def rows_of(array):
        if array.ndim == 3:
            return pl.BlockSpec((array.shape[0], 8, array.shape[2]), lambda i: (0, i, 0))
        if array.shape[0] == 32:
            return pl.BlockSpec((8, array.shape[1]), lambda i: (i, 0))
        return pl.BlockSpec(array.shape, lambda i: (0, 0))

    flat_params = [array for group in params for array in group]
    specs = [rows_of(array) for array in flat_params]
    done = pl.pallas_call(
        finish,
        grid=(4,),
        out_shape=[shape((ROWS, D), f32)] * 2 + [shape(v.shape, f32) for v in flat_params],
        in_specs=[big, big] + [rows_of(v) for v in grads] + specs,
        out_specs=[big, big] + specs,
        name="finish",
    )(mixed.reshape(ROWS, D), tg.reshape(ROWS, D), *grads, *flat_params)
    news = [done[2 + 3 * k : 5 + 3 * k] for k in range(6)]
    return (
        done[0].reshape(tokens.shape),
        done[1].reshape(tokens.shape),
        *news[0],
        *(v.T for v in news[1]),
        *news[2],
        *(v.T for v in news[3]),
        *news[4],
        *news[5],
    )


def solution(mesh):
    rows = P("dp", "seq", None)
    stack = P(None, ("dp", "seq"), "mp")
    flat = P("mp", ("dp", "seq"))
    thin = P(None, ("dp", "seq"))
    groups = (stack,) * 3 + (flat,) * 3 + (stack,) * 3 + (flat,) * 3 + (thin,) * 6
    return jax.shard_map(
        local,
        mesh=mesh,
        in_specs=(rows, rows) + groups,
        out_specs=(rows, rows) + groups,
        check_vma=False,
    )
```

```python
import jax
import jax.numpy as jnp
from jax import lax
from jax.experimental import pallas as pl
from jax.experimental.pallas import tpu as pltpu
from jax.sharding import PartitionSpec as P

STEP = 10

beta_one = 0.9
beta_two = 0.95
eps_adam = 1e-08
eps_norm = 1e-05
rate_matrix = 0.05
rate_small = 0.3
decay_matrix = 0.1

MESH = pl.DeviceIdType.MESH
bf16 = jnp.bfloat16
f32 = jnp.float32

ROWS = 512
CHUNK = 128
D = 1024
CH = 256
FF = 1152
IN0, SM0, OUT0, GU0, DN0, COLS = 0, 768, 896, 1152, 3456, 4608
GRAD_OUT0 = 768


def adamw(master, first, second, grad, rate, decay):
    moment = beta_one * first + (1.0 - beta_one) * grad
    square = beta_two * second + (1.0 - beta_two) * grad * grad
    moment_hat = moment / (1.0 - beta_one**STEP)
    square_hat = square / (1.0 - beta_two**STEP)
    renewed = master - rate * (moment_hat / (jnp.sqrt(square_hat) + eps_adam) + decay * master)
    return (renewed, moment, square)


def rms_scale(values):
    return lax.rsqrt(jnp.mean(values * values, axis=-1, keepdims=True) + eps_norm)


def dot_nn(a, b):
    return jnp.dot(a, b, preferred_element_type=f32)


def dot_nt(a, b):
    return lax.dot_general(a, b, (((1,), (1,)), ((), ())), preferred_element_type=f32)


def dot_tn(a, b):
    return lax.dot_general(a, b, (((0,), (0,)), ((), ())), preferred_element_type=f32)


N_SEMS = 192


def kernel(
    tok_h,
    cot_h,
    w_in,
    w_out,
    w_gu,
    w_dn,
    w_conv,
    w_gain,
    mixed_o,
    tg_o,
    g_in,
    g_out,
    g_gu,
    g_dn,
    small_o,
    tok,
    cot,
    htok,
    square,
    W,
    G,
    RC,
    RX,
    T,
    RZ,
    act1,
    ulow,
    act2,
    rlow,
    hid,
    GG,
    b_s,
    c_s,
    x_s,
    conv_s,
    xext,
    gext,
    hlow,
    gated,
    GB,
    c_after,
    smw,
    SM,
    SMR,
    PY,
    RY,
    OWN,
    res_s,
    own_tok,
    mixrow,
    tgrow,
    ssem,
    rsem,
    lsem,
):
    z = lax.axis_index("dp")
    seq = lax.axis_index("seq")
    y = lax.axis_index("mp")
    x = seq // 2
    c = lax.rem(seq, 2)
    oc = 1 - c

    def near(value, step):
        return lax.rem(value + step, 4)

    def to_x(step):
        return (z, near(x, step) * 2 + c, y)

    def to_z(step):
        return (near(z, step), seq, y)

    def to_y(step):
        return (z, seq, near(y, step))

    to_core = (z, x * 2 + oc, y)
    to_next = (z, lax.rem(seq + 1, 8), y)
    to_prev = (z, lax.rem(seq + 7, 8), y)

    counter = [0]
    pending = []

    def send(src, dst, where):
        i = counter[0]
        assert i < N_SEMS
        counter[0] += 1
        copy = pltpu.make_async_remote_copy(
            src, dst, ssem.at[i], rsem.at[i], device_id=where, device_id_type=MESH
        )
        copy.start()
        pending.append(copy)
        return copy

    def arrived(copies):
        for copy in copies:
            copy.wait_recv()

    barrier = pltpu.get_barrier_semaphore()
    peers = [to_core, to_prev] + [(z, lax.rem(seq + 1, 8), k) for k in range(4)]
    for step in (1, 2, 3):
        peers += [to_x(step), to_z(step), to_y(step)]
    for peer in peers:
        pl.semaphore_signal(barrier, inc=1, device_id=peer, device_id_type=MESH)
    load_tok = pltpu.make_async_copy(tok_h, tok, lsem.at[2])
    load_tok.start()
    load_cot = pltpu.make_async_copy(cot_h, cot, lsem.at[3])
    load_cot.start()

    for k in range(3):
        W[z, x, c, :, CH * k : CH * k + CH] = w_in[k].astype(bf16)
    W[z, x, c, :, OUT0:GU0] = w_out[...].astype(bf16)
    square[...] = jnp.zeros((128, 128), f32)
    square[0:3, 0:32] = w_conv[...]
    square[3:5, 0:32] = w_gain[...]
    W[z, x, c, :, SM0:OUT0] = square[...].T[0:32].astype(bf16)
    pl.semaphore_wait(barrier, len(peers))

    def ag_one(lo, mid, hi):
        a, b = pl.ds(lo, mid - lo), pl.ds(mid, hi - mid)
        src_a, src_b = W.at[z, x, c, :, a], W.at[z, x, c, :, b]
        return (
            [send(src_a, src_a, to_x(s)) for s in (1, 3, 2)],
            [send(src_b, src_b, to_z(s)) for s in (1, 3, 2)],
        )

    def ag_two(copies, lo, mid, hi):
        a, b = pl.ds(lo, mid - lo), pl.ds(mid, hi - mid)
        src_a, src_b = W.at[z, :, c, :, a], W.at[:, x, c, :, b]
        arrived(copies[0])
        first = [send(src_a, src_a, to_z(s)) for s in (1, 3)]
        arrived(copies[1])
        second = [send(src_b, src_b, to_x(s)) for s in (1, 3)]
        return first, second, [send(src_a, src_a, to_core), send(src_b, src_b, to_core)]

    def ag_pass(copies, lo, mid, hi):
        core = copies[2]
        a, b = pl.ds(lo, mid - lo), pl.ds(mid, hi - mid)
        low, high = pl.ds(0, 2), pl.ds(2, 2)
        out = []
        for s, half in ((1, low), (3, high)):
            i = 0 if s == 1 else 1
            arrived([copies[0][i]])
            src = W.at[near(z, 4 - s), half, c, :, a]
            out += [send(src, src, to_z(s))]
            arrived([copies[1][i]])
            src = W.at[half, near(x, 4 - s), c, :, b]
            out += [send(src, src, to_x(s))]
            src = W.at[near(z, 4 - s), :, c, :, a]
            core = core + [send(src, src, to_core)]
            src = W.at[:, near(x, 4 - s), c, :, b]
            core = core + [send(src, src, to_core)]
        return out, core

    def ag_three(copies, lo, mid, hi):
        a, b = pl.ds(lo, mid - lo), pl.ds(mid, hi - mid)
        arrived(copies[0])
        src_a, src_b = W.at[near(z, 2), :, c, :, a], W.at[:, near(x, 2), c, :, b]
        return copies[1] + [send(src_a, src_a, to_core), send(src_b, src_b, to_core)]

    def ag_two_direct(copies, lo, mid, hi):
        a, b = pl.ds(lo, mid - lo), pl.ds(mid, hi - mid)
        src_a, src_b = W.at[z, :, c, :, a], W.at[:, x, c, :, b]
        arrived(copies[0])
        first = [send(src_a, src_a, to_z(s)) for s in (1, 3, 2)]
        arrived(copies[1])
        second = [send(src_b, src_b, to_x(s)) for s in (1, 3, 2)]
        core = [send(src_a, src_a, to_core), send(src_b, src_b, to_core)]
        return first, second, core

    def ag_three_direct(copies, lo, mid, hi):
        a, b = pl.ds(lo, mid - lo), pl.ds(mid, hi - mid)
        first, second, core = copies
        for k, s in enumerate((1, 3, 2)):
            arrived([first[k]])
            src = W.at[near(z, 4 - s), :, c, :, a]
            core = core + [send(src, src, to_core)]
            arrived([second[k]])
            src = W.at[:, near(x, 4 - s), c, :, b]
            core = core + [send(src, src, to_core)]
        return core

    g0 = (IN0, 512, OUT0)
    go = (OUT0, OUT0 + 128, GU0)
    g1 = (GU0, GU0 + 1152, DN0)
    g2 = (DN0, DN0 + 640, COLS)
    ag0 = ag_one(*g0)
    ago = ag_one(*go)
    halo = [
        send(tok_h.at[pl.ds(ROWS - 16, 16)], htok.at[0], to_next),
        send(tok_h.at[pl.ds(0, 16)], htok.at[1], to_prev),
    ]
    for t in range(9):
        for k in range(2):
            at = GU0 + 256 * t + 128 * k
            W[z, x, c, :, at : at + 128] = w_gu[k, :, 128 * t : 128 * t + 128].astype(bf16)
    W[z, x, c, :, DN0:COLS] = w_dn[...].astype(bf16)
    ag0 = ag_two_direct(ag0, *g0)
    ago = ag_two_direct(ago, *go)
    ag1 = ag_one(*g1)
    ag2 = ag_one(*g2)
    load_tok.wait()
    mine = pl.ds(pl.multiple_of(y * CHUNK, CHUNK), CHUNK)
    own_tok[...] = tok[mine]
    for i in range(4):
        here = slice(CHUNK * i, CHUNK * i + CHUNK)
        v = tok[here]
        tok[here] = v * rms_scale(v)
    ag0 = ag_three_direct(ag0, *g0)
    ag1 = ag_two(ag1, *g1)
    ag2 = ag_two(ag2, *g2)
    load_cot.wait()
    for r in range(0, ROWS, 128):
        ulow[r : r + 128] = cot[r : r + 128].astype(bf16)
    ago = ag_three_direct(ago, *go)
    arrived(ag0)

    def weights(lo, n):
        return W[:, :, :, :, pl.ds(lo, n)].reshape(D, n)

    def weight_rows(block, lo, n):
        return W[block, :, :, :, pl.ds(lo, n)].reshape(256, n)

    smw[...] = weights(SM0, 128).astype(f32).T[:8]
    gain_one = smw[3:4]
    gain_two = smw[4:5]
    own_channels = pl.ds(pl.multiple_of(y * CH, CH), CH)
    taps = smw[:, own_channels]
    tap0, tap1, tap2 = taps[0:1], taps[1:2], taps[2:3]

    for i in range(4):
        act1[CHUNK * i + 16 : CHUNK * i + 144] = (tok[CHUNK * i : CHUNK * i + CHUNK] * gain_one).astype(bf16)
    arrived(halo)
    for i in range(2):
        v = htok[i]
        at = i * (ROWS + 16)
        act1[at : at + 16] = (v * rms_scale(v) * gain_one).astype(bf16)
    bgate = dot_nn(act1[0 : ROWS + 16], weights(0, CH))
    xvalue = dot_nn(act1[0 : ROWS + 16], weights(2 * CH, CH))
    xext[...] = (bgate * xvalue).astype(bf16).astype(f32)
    b_s[...] = bgate[16:]
    x_s[...] = xvalue[16:]
    xext[0:16] = jnp.where(seq > 0, xext[0:16], 0.0)
    cgate = dot_nn(act1[16:], weights(CH, CH))
    c_s[...] = cgate[0:ROWS]
    c_after[...] = cgate[ROWS:]
    conv_s[...] = (
        tap0 * xext[14 : ROWS + 14] + tap1 * xext[15 : ROWS + 15] + tap2 * xext[16 : ROWS + 16]
    )
    gated[...] = (c_s[...] * conv_s[...]).astype(bf16)
    arrived(ago)

    def chunk_rows(step):
        return pl.ds(pl.multiple_of(near(y, step) * CHUNK, CHUNK), CHUNK)

    def partial(which, steps, values, lo, n):
        for block in range(4):
            part = dot_nt(values, weight_rows(block, lo, n))
            cols = slice(block * 256, block * 256 + 256)
            for k, step in enumerate(steps):
                piece = part[CHUNK * k : CHUNK * k + CHUNK]
                if step == 0:
                    OWN[which, :, cols] = piece
                else:
                    PY[which, step - 1, :, cols] = piece.astype(bf16)
        return [
            send(PY.at[which, step - 1], RY.at[which, step - 1], to_y(step))
            for step in steps
            if step
        ]

    half = CHUNK // 2
    low_half, high_half = pl.ds(0, half), pl.ds(half, half)

    def part_of(which, slot, rows, where):
        return send(PY.at[which, slot, rows], RY.at[which, slot, rows], where)

    def rs_y(which, source, lo, n, against=None):
        def block_of(step):
            return source[chunk_rows(step)]

        for step in (2, 1, 3, 0):
            values = block_of(step)
            for block in range(4):
                part = dot_nt(values, weight_rows(block, lo, n))
                cols = slice(block * 256, block * 256 + 256)
                if against is not None:
                    SM[0, 3:4, cols] += jnp.sum(
                        part * against[chunk_rows(step), cols], axis=0, keepdims=True
                    )
                if step == 0:
                    OWN[which, :, cols] = part
                else:
                    PY[which, step - 1, :, cols] = part.astype(bf16)
            if step == 2:
                relay = (
                    part_of(which, 1, low_half, to_y(1)),
                    part_of(which, 1, high_half, to_y(3)),
                )
            elif step == 1:
                direct = [part_of(which, 0, high_half, to_y(1))]
            elif step == 3:
                direct += [part_of(which, 2, low_half, to_y(3))]
        return relay, direct

    def rs_y_pass(which, state):
        relay, direct = state
        out = list(direct)
        for k, (slot, rows, where) in enumerate(
            ((0, slice(0, half), to_y(1)), (2, slice(half, CHUNK), to_y(3)))
        ):
            arrived([relay[k]])
            PY[which, slot, rows] = (
                PY[which, slot, rows].astype(f32) + RY[which, 1, rows].astype(f32)
            ).astype(bf16)
            out += [part_of(which, slot, low_half if k == 0 else high_half, where)]
        return out

    def summed_relayed(which, copies):
        arrived(copies)
        return OWN[which] + RY[which, 0].astype(f32) + RY[which, 2].astype(f32)

    def summed(which, copies):
        arrived(copies)
        return (
            OWN[which]
            + RY[which, 0].astype(f32)
            + RY[which, 1].astype(f32)
            + RY[which, 2].astype(f32)
        )

    def ag_y(src, slot):
        return (send(src, slot(y), to_y(1)), send(src, slot(y), to_y(3)))

    def ag_y_pass(copies, slot):
        arrived(copies[:1])
        left = slot(near(y, 3)).at[pl.ds(0, half)]
        out = [send(left, left, to_y(1))]
        arrived(copies[1:])
        right = slot(near(y, 1)).at[pl.ds(half, half)]
        return out + [send(right, right, to_y(3))]

    rs = rs_y(0, gated, OUT0, CH)
    ag1 = ag_pass(ag1, *g1)
    ag2 = ag_pass(ag2, *g2)
    rs = rs_y_pass(0, rs)
    ag1 = ag_three(ag1, *g1)
    ag2 = ag_three(ag2, *g2)

    own_rows = chunk_rows(0)
    resid = own_tok[...] + summed_relayed(0, rs)
    res_s[...] = resid
    act2[y] = (resid * rms_scale(resid) * gain_two).astype(bf16)
    def act2_slot(i):
        return act2.at[i]

    ag_act2 = ag_y(act2.at[y], act2_slot)
    arrived(ag1)
    arrived(ag2)

    def ffn_part(acts, ups, rows, f_lo, n):
        gu = dot_nn(acts, weights(GU0 + 2 * f_lo, 2 * n))
        gh = dot_nn(ups, weights(DN0 + f_lo, n))
        for j in range(n // 128):
            gate = gu[:, 256 * j : 256 * j + 128]
            up = gu[:, 256 * j + 128 : 256 * j + 256]
            grad = gh[:, 128 * j : 128 * j + 128]
            sig = jax.nn.sigmoid(gate)
            swish = gate * sig
            hidden = (swish * up).astype(bf16)
            grad_gate = (grad * up * sig * (1.0 + gate * (1.0 - sig))).astype(bf16)
            grad_up = (grad * swish).astype(bf16)
            for k, here in enumerate(rows):
                piece = slice(CHUNK * k, CHUNK * k + CHUNK)
                hid[here, pl.ds(f_lo + 128 * j, 128)] = hidden[piece]
                GG[here, pl.ds(2 * f_lo + 256 * j, 128)] = grad_gate[piece]
                GG[here, pl.ds(2 * f_lo + 256 * j + 128, 128)] = grad_up[piece]

    def stacked(parts):
        return parts[0] if len(parts) == 1 else jnp.concatenate(parts, axis=0)

    rs = []
    for steps in ((0,), (1, 3), (2,)):
        if steps == (1, 3):
            ag_act2 = ag_y_pass(ag_act2, act2_slot)
        if steps == (2,):
            arrived(ag_act2)
        rows = [chunk_rows(step) for step in steps]
        acts = stacked([act2[near(y, step)] for step in steps])
        ups = stacked([ulow[here] for here in rows])

        @pl.loop(0, 4)
        def _(t):
            ffn_part(acts, ups, rows, pl.multiple_of(t * 256, 256), 256)

        ffn_part(acts, ups, rows, 1024, 128)
        rs += partial(1, steps, stacked([GG[here] for here in rows]), GU0, 2 * FF)

    def weight_grad(left, right, lo, n):
        for block in range(4):
            values = left(block)
            for start in range(0, n, 256):
                width = min(256, n - start)
                part = dot_tn(values, right[:, pl.ds(start, width)])
                G[block, :, :, :, pl.ds(lo + start, width)] = part.astype(bf16).reshape(
                    4, 2, 32, width
                )

    def rs_core(lo, hi):
        cols = pl.ds(lo, hi - lo)
        return [send(G.at[:, :, oc, :, cols], RC.at[:, :, :, cols], to_core)]

    def rs_one(copies, lo, mid, hi):
        arrived(copies)
        cols = pl.ds(lo, hi - lo)

        @pl.loop(0, 4)
        def _(i):
            for j in range(4):
                G[i, j, c, :, cols] = (
                    G[i, j, c, :, cols].astype(f32) + RC[i, j, :, cols].astype(f32)
                ).astype(bf16)

        a, b = pl.ds(lo, mid - lo), pl.ds(mid, hi - mid)
        out = []
        for s in (1, 3, 2):
            out += [send(G.at[:, near(x, s), c, :, a], RX.at[s - 1, :, :, a], to_x(s))]
            out += [send(G.at[near(z, s), :, c, :, b], RX.at[s - 1, :, :, b], to_z(s))]
        return out

    def rs_two(copies, lo, mid, hi):
        arrived(copies)
        a, b = pl.ds(lo, mid - lo), pl.ds(mid, hi - mid)

        @pl.loop(0, 4)
        def _(i):
            T[i, :, a] = (
                G[i, x, c, :, a].astype(f32)
                + RX[0, i, :, a].astype(f32)
                + RX[1, i, :, a].astype(f32)
                + RX[2, i, :, a].astype(f32)
            ).astype(bf16)
            T[i, :, b] = (
                G[z, i, c, :, b].astype(f32)
                + RX[0, i, :, b].astype(f32)
                + RX[1, i, :, b].astype(f32)
                + RX[2, i, :, b].astype(f32)
            ).astype(bf16)

        out = []
        for s in (1, 3, 2):
            out += [send(T.at[near(z, s), :, a], RZ.at[s - 1, :, a], to_z(s))]
            out += [send(T.at[near(x, s), :, b], RZ.at[s - 1, :, b], to_x(s))]
        return out

    def rs_end(lo, n, mid):
        cols = pl.ds(lo, n)
        mine = z if lo < mid else x
        return (
            T[mine, :, cols].astype(f32)
            + RZ[0, :, cols].astype(f32)
            + RZ[1, :, cols].astype(f32)
            + RZ[2, :, cols].astype(f32)
        )

    gi = (IN0, 512, 1024)
    weight_grad(
        lambda i: act2[:, :, i * 256 : i * 256 + 256].reshape(ROWS, 256), GG, GU0, 2 * FF
    )
    r_gu = rs_core(GU0, DN0)

    back_two = summed(1, rs)
    resid = res_s[...]
    scale_two = rms_scale(resid)
    normed = resid * scale_two
    SM[0] = jnp.zeros((8, D), f32)
    SM[0, 4:5] = jnp.sum(back_two * normed, axis=0, keepdims=True)
    scaled = back_two * gain_two
    grad_resid = cot[own_rows] + scale_two * (
        scaled - normed * jnp.mean(scaled * normed, axis=-1, keepdims=True)
    )
    rlow[y] = grad_resid.astype(bf16)

    def rlow_slot(i):
        return rlow.at[i]

    low_at = counter[0]
    counter[0] += 4
    low_halo = [
        pltpu.make_async_remote_copy(
            rlow.at[0, pl.ds(0, 16)],
            hlow,
            ssem.at[low_at + k],
            rsem.at[low_at],
            device_id=(z, lax.rem(seq + 7, 8), k),
            device_id_type=MESH,
        )
        for k in range(4)
    ]

    @pl.when(y == 0)
    def _():
        for copy in low_halo:
            copy.start()

    ag_rlow = ag_y(rlow.at[y], rlow_slot)
    OWN[1] = grad_resid

    rs_ffn = rs_y(2, hid, DN0, FF)
    r_gu = rs_one(r_gu, *g1)
    ag_rlow = ag_y_pass(ag_rlow, rlow_slot)
    weight_grad(lambda i: ulow[:, i * 256 : i * 256 + 256], hid, DN0, FF)
    r_dn = rs_core(DN0, COLS)
    rs_ffn = rs_y_pass(2, rs_ffn)

    arrived(ag_rlow)

    r_dn = rs_one(r_dn, *g2)

    low = rlow[...].reshape(ROWS, D)
    grad_gated = dot_nn(low, weights(OUT0, CH))
    gext[0:ROWS] = (grad_gated * c_s[...]).astype(bf16).astype(f32)
    low_halo[0].wait_recv()
    after = (dot_nn(hlow[...], weights(OUT0, CH)) * c_after[...]).astype(bf16).astype(f32)
    gext[ROWS : ROWS + 8] = jnp.where(seq < 7, after[0:8], 0.0)
    GB[:, CH : 2 * CH] = (grad_gated * conv_s[...]).astype(bf16)
    grad_mixed = tap2 * gext[0:ROWS] + tap1 * gext[1 : ROWS + 1] + tap0 * gext[2 : ROWS + 2]
    GB[:, 0:CH] = (grad_mixed * x_s[...]).astype(bf16)
    GB[:, 2 * CH : 3 * CH] = (grad_mixed * b_s[...]).astype(bf16)

    rs = rs_y(3, GB, IN0, 3 * CH, tok)
    grad_conv = gext[0:ROWS]
    for k in range(3):
        row = jnp.sum(grad_conv * xext[14 + k : ROWS + 14 + k], axis=0, keepdims=True)
        SM[0, k : k + 1, own_channels] = row
    mixrow[...] = (res_s[...] + summed_relayed(2, rs_ffn)).astype(bf16)

    def mixed_slot(i):
        return mixed_o.at[i]

    ag_mixed = ag_y(mixrow, mixed_slot)
    local_mixed = pltpu.make_async_copy(mixrow, mixed_o.at[y], lsem.at[0])
    local_mixed.start()


    sm = [send(SM.at[0], SMR.at[0], to_core)]
    weight_grad(
        lambda i: rlow[:, :, i * 256 : i * 256 + 256].reshape(ROWS, 256), gated, GRAD_OUT0, CH
    )
    weight_grad(lambda i: act1[16 : ROWS + 16, i * 256 : i * 256 + 256], GB, IN0, 3 * CH)
    arrived(sm)
    SM[1] = SM[0] + SMR[0]
    sm = [send(SM.at[1], SMR.at[s], to_x(s)) for s in (1, 3, 2)]
    r_in = rs_core(IN0, 1024)
    rs = rs_y_pass(3, rs)

    r_in = rs_one(r_in, *gi)

    back_one = summed_relayed(3, rs)
    scale_one = rms_scale(own_tok[...])
    normed = tok[own_rows]
    scaled = back_one * gain_one
    tgrow[...] = (
        OWN[1]
        + scale_one * (scaled - normed * jnp.mean(scaled * normed, axis=-1, keepdims=True))
    ).astype(bf16)

    def tg_slot(i):
        return tg_o.at[i]

    ag_tg = ag_y(tgrow, tg_slot)
    local_tg = pltpu.make_async_copy(tgrow, tg_o.at[y], lsem.at[1])
    local_tg.start()

    arrived(sm)
    SM[2] = SM[1] + SMR[1] + SMR[2] + SMR[3]
    sm = [send(SM.at[2], SMR.at[3 + s], to_z(s)) for s in (1, 3, 2)]
    ag_mixed = ag_y_pass(ag_mixed, mixed_slot)
    r_gu = rs_two(r_gu, *g1)
    r_dn = rs_two(r_dn, *g2)
    arrived(sm)
    SMR[7] = SM[2] + SMR[4] + SMR[5] + SMR[6]
    sm = [send(SMR.at[7], SMR.at[7 + s], to_y(s)) for s in (1, 3, 2)]

    arrived(r_dn)
    g_dn[:, 0:640] = rs_end(DN0, 640, g2[1])
    g_dn[:, 640:1152] = rs_end(DN0 + 640, 512, g2[1])

    r_in = rs_two(r_in, *gi)

    ag_tg = ag_y_pass(ag_tg, tg_slot)
    arrived(r_gu)
    for t in range(9):
        g_gu[0, :, 128 * t : 128 * t + 128] = rs_end(GU0 + 256 * t, 128, g1[1])
        g_gu[1, :, 128 * t : 128 * t + 128] = rs_end(GU0 + 256 * t + 128, 128, g1[1])

    arrived(r_in)
    for k in range(3):
        g_in[k] = rs_end(IN0 + CH * k, CH, gi[1])
    g_out[...] = rs_end(GRAD_OUT0, CH, gi[1])

    arrived(sm)

    def term(j):
        return SMR[7 + lax.rem(y - j + 4, 4)]

    shard_at = z * 8 + seq
    SMR[0] = ((term(0) + term(1)) + term(2)) + term(3)
    four = SMR[0, :, pl.ds(pl.multiple_of(shard_at // 4 * 128, 128), 128)]
    place = lax.rem(shard_at, 4)
    mine = four[:, 0:32]
    for k in range(1, 4):
        mine = jnp.where(place == k, four[:, 32 * k : 32 * k + 32], mine)
    small_o[...] = mine

    arrived(ag_mixed)
    arrived(ag_tg)
    local_mixed.wait()
    local_tg.wait()
    for copy in pending:
        copy.wait_send()

    @pl.when(y == 0)
    def _():
        for copy in low_halo:
            copy.wait_send()


def finish(*refs):
    refs[25][...] = refs[0][...].astype(f32)
    refs[26][...] = refs[1][...].astype(f32)
    small = refs[6][...]
    grads = [ref[...] for ref in refs[2:6]] + [small[0:3], small[3:5]]
    for k, grad in enumerate(grads):
        rate, decay = (rate_matrix, decay_matrix) if k < 4 else (rate_small, 0.0)
        group = refs[7 + 3 * k : 10 + 3 * k]
        new = adamw(*(ref[...] for ref in group), grad, rate, decay)
        for ref, value in zip(refs[27 + 3 * k : 30 + 3 * k], new):
            ref[...] = value


def local(
    tokens,
    cotangent,
    in_weight,
    in_first,
    in_second,
    out_weight,
    out_first,
    out_second,
    gu_weight,
    gu_first,
    gu_second,
    down_weight,
    down_first,
    down_second,
    conv_weight,
    conv_first,
    conv_second,
    norm_gains,
    gains_first,
    gains_second,
):
    vmem = pl.BlockSpec(memory_space=pltpu.VMEM)
    hbm = pl.BlockSpec(memory_space=pl.ANY)
    shape = jax.ShapeDtypeStruct
    mixed, tg, grad_in, grad_out, grad_gu, grad_dn, grad_small = pl.pallas_call(
        kernel,
        out_shape=(
            shape((4, CHUNK, D), bf16),
            shape((4, CHUNK, D), bf16),
            shape((3, 32, CH), f32),
            shape((32, CH), f32),
            shape((2, 32, FF), f32),
            shape((32, FF), f32),
            shape((8, 32), f32),
        ),
        in_specs=[hbm] * 2 + [vmem] * 6,
        out_specs=(hbm, hbm, vmem, vmem, vmem, vmem, vmem),
        scratch_shapes=[
            pltpu.VMEM((ROWS, D), f32),
            pltpu.VMEM((ROWS, D), f32),
            pltpu.VMEM((2, 16, D), f32),
            pltpu.VMEM((128, 128), f32),
            pltpu.VMEM((4, 4, 2, 32, COLS), bf16),
            pltpu.VMEM((4, 4, 2, 32, COLS), bf16),
            pltpu.VMEM((4, 4, 32, COLS), bf16),
            pltpu.VMEM((3, 4, 32, COLS), bf16),
            pltpu.VMEM((4, 32, COLS), bf16),
            pltpu.VMEM((3, 32, COLS), bf16),
            pltpu.VMEM((ROWS + 32, D), bf16),
            pltpu.VMEM((ROWS, D), bf16),
            pltpu.VMEM((4, CHUNK, D), bf16),
            pltpu.VMEM((4, CHUNK, D), bf16),
            pltpu.VMEM((ROWS, FF), bf16),
            pltpu.VMEM((ROWS, 2 * FF), bf16),
            pltpu.VMEM((ROWS, CH), f32),
            pltpu.VMEM((ROWS, CH), f32),
            pltpu.VMEM((ROWS, CH), f32),
            pltpu.VMEM((ROWS, CH), f32),
            pltpu.VMEM((ROWS + 16, CH), f32),
            pltpu.VMEM((ROWS + 8, CH), f32),
            pltpu.VMEM((16, D), bf16),
            pltpu.VMEM((ROWS, CH), bf16),
            pltpu.VMEM((ROWS, 3 * CH), bf16),
            pltpu.VMEM((16, CH), f32),
            pltpu.VMEM((8, D), f32),
            pltpu.VMEM((3, 8, D), f32),
            pltpu.VMEM((11, 8, D), f32),
            pltpu.VMEM((4, 3, CHUNK, D), bf16),
            pltpu.VMEM((4, 3, CHUNK, D), bf16),
            pltpu.VMEM((4, CHUNK, D), f32),
            pltpu.VMEM((CHUNK, D), f32),
            pltpu.VMEM((CHUNK, D), f32),
            pltpu.VMEM((CHUNK, D), bf16),
            pltpu.VMEM((CHUNK, D), bf16),
            pltpu.SemaphoreType.DMA((N_SEMS,)),
            pltpu.SemaphoreType.DMA((N_SEMS,)),
            pltpu.SemaphoreType.DMA((4,)),
        ],
        name="block_step",
        compiler_params=pltpu.CompilerParams(
            collective_id=0, has_side_effects=True, vmem_limit_bytes=62 << 20
        ),
    )(
        tokens.reshape(ROWS, D),
        cotangent.reshape(ROWS, D),
        in_weight,
        out_weight.T,
        gu_weight,
        down_weight.T,
        conv_weight,
        norm_gains,
    )
    params = (
        (in_weight, in_first, in_second),
        (out_weight.T, out_first.T, out_second.T),
        (gu_weight, gu_first, gu_second),
        (down_weight.T, down_first.T, down_second.T),
        (conv_weight, conv_first, conv_second),
        (norm_gains, gains_first, gains_second),
    )
    grads = (grad_in, grad_out, grad_gu, grad_dn, grad_small)
    big = pl.BlockSpec((CHUNK, D), lambda i: (i, 0))

    def rows_of(array):
        if array.ndim == 3:
            return pl.BlockSpec((array.shape[0], 8, array.shape[2]), lambda i: (0, i, 0))
        if array.shape[0] == 32:
            return pl.BlockSpec((8, array.shape[1]), lambda i: (i, 0))
        return pl.BlockSpec(array.shape, lambda i: (0, 0))

    flat_params = [array for group in params for array in group]
    specs = [rows_of(array) for array in flat_params]
    done = pl.pallas_call(
        finish,
        grid=(4,),
        out_shape=[shape((ROWS, D), f32)] * 2 + [shape(v.shape, f32) for v in flat_params],
        in_specs=[big, big] + [rows_of(v) for v in grads] + specs,
        out_specs=[big, big] + specs,
        name="finish",
    )(mixed.reshape(ROWS, D), tg.reshape(ROWS, D), *grads, *flat_params)
    news = [done[2 + 3 * k : 5 + 3 * k] for k in range(6)]
    return (
        done[0].reshape(tokens.shape),
        done[1].reshape(tokens.shape),
        *news[0],
        *(v.T for v in news[1]),
        *news[2],
        *(v.T for v in news[3]),
        *news[4],
        *news[5],
    )


def solution(mesh):
    rows = P("dp", "seq", None)
    stack = P(None, ("dp", "seq"), "mp")
    flat = P("mp", ("dp", "seq"))
    thin = P(None, ("dp", "seq"))
    groups = (stack,) * 3 + (flat,) * 3 + (stack,) * 3 + (flat,) * 3 + (thin,) * 6
    return jax.shard_map(
        local,
        mesh=mesh,
        in_specs=(rows, rows) + groups,
        out_specs=(rows, rows) + groups,
        check_vma=False,
    )
```
